512 devices in a mesh: res: 128 (over z, y, core), dp: 4 (over x).
Axes of the slice: x: 4, y: 8, z: 8, core: 2. Of those that a mesh axis runs over, the one named last changes fastest.
Arguments:
- aligned_chain_features: bfloat16 [512, 256, 256], P('dp', 'res'), parts along dimension 0, may hold values from -6 to 6
- pair_representation_state: bfloat16 [1024, 256, 128], P(('dp', 'res')), parts along dimension 0, may hold values from -6 to 6
- gap_block_flags: int32 [512, 2], P('dp'), parts along dimension 0, may hold values from 0 to 1, as said below
- pair_norm_gain: float32 [128], replicated, may hold values from 0.1 to 1.9
- pair_head_weight: bfloat16 [128, 8], replicated, may hold values from -0.5 to 0.5
- horizontal_scaling_factor: float32 [256], replicated, may hold values from 0.1 to 1.9
- row_input_weight: bfloat16 [256, 1024], replicated, may hold values from -2 to 2
- horizontal_final_matrix: bfloat16 [256, 256], replicated, may hold values from -0.375 to 0.375
- vertical_scaling_factor: float32 [256], replicated, may hold values from 0.1 to 1.9
- column_input_weight: bfloat16 [256, 1024], replicated, may hold values from -2 to 2
- vertical_final_matrix: bfloat16 [256, 256], replicated, may hold values from -0.375 to 0.375
- feedforward_scaling_factor: float32 [256], replicated, may hold values from 0.1 to 1.9
- feedforward_widen_matrix: bfloat16 [256, 1024], replicated, may hold values from -0.375 to 0.375
- feedforward_shrink_matrix: bfloat16 [1024, 256], replicated, may hold values from -0.1875 to 0.1875
Outputs:
- msa_out: bfloat16 [512, 256, 256], P('dp', 'res'), parts along dimension 0
The draws below stay inside these ranges and needn't reach their ends.
There are 4 independent parts, one for each index of `dp`. The reference program is written for one: setup_inputs(seed, part) draws one part's arguments, and reference() takes and returns one part's arrays. A program takes and returns all parts, laid end to end along the dimension named above; an argument that names none is the same for every part. Nothing has to cross between parts.
Inputs may be any that keep to these rules, and one draw needn't show every extreme that they name: `gap_block_flags`: row 0 holds no gap block, and every row has at least one block that is not a gap.
All inputs are finite; a program needn't handle non-finite values.
Results may differ from the reference program's by a relative error of at most 0.015.
The reference program's roundings to bfloat16 on the way count: a program that leaves them out, or rounds other values in their place, can miss the bound.
Values may be sent and summed in bfloat16 or wider, within the bound.
A program may use at most 64 MiB of HBM per device.

```python
import jax
import jax.numpy as jnp
from jax import lax

FEATURE_DEPTH = 256
FOCUS_COUNT = 8
PER_HEADER_DEPTH = 32
CZ = 128
GROUPED_CHAINS = 128
WINDOW_SITES_N = 256
BLOCK = 128
WIDENED_UNITS = 1024


def draw_gap_block_flags(key, part):
    key = jax.random.fold_in(key, 11)
    key_level, key_rolls, key_keep = jax.random.split(key, 3)
    block_total = WINDOW_SITES_N // BLOCK
    gap_level = jax.random.randint(key_level, (GROUPED_CHAINS, 1), 0, 90)
    dice_rolls = jax.random.randint(key_rolls, (GROUPED_CHAINS, block_total), 0, 100)
    kept_block = jax.random.randint(key_keep, (GROUPED_CHAINS, 1), 0, block_total)
    block_ids = jnp.arange(block_total, dtype=jnp.int32)[None, :]
    seq_ids = jnp.arange(GROUPED_CHAINS, dtype=jnp.int32)[:, None]
    gap_flags = jnp.where(dice_rolls < gap_level, 1, 0)
    gap_flags = jnp.where(block_ids == kept_block, 0, gap_flags)
    gap_flags = jnp.where(seq_ids == 0, 0, gap_flags)
    return gap_flags.astype(jnp.int32)


def draw_row_input_weight(key, part):
    key = jax.random.fold_in(key, 23)
    random_seed_root = jax.random.fold_in(key, 0)
    random_seed_draw = jnp.clip(jax.random.normal(random_seed_root, (FEATURE_DEPTH, 4, FOCUS_COUNT, PER_HEADER_DEPTH), jnp.float32), -3.0, 3.0)
    return (random_seed_draw * FEATURE_DEPTH ** (-0.5)).reshape(FEATURE_DEPTH, 4 * FOCUS_COUNT * PER_HEADER_DEPTH).astype(jnp.bfloat16)


def draw_column_input_weight(key, part):
    key = jax.random.fold_in(key, 37)
    random_seed_root = jax.random.fold_in(key, 0)
    random_seed_draw = jnp.clip(jax.random.normal(random_seed_root, (FEATURE_DEPTH, 4, FOCUS_COUNT, PER_HEADER_DEPTH), jnp.float32), -3.0, 3.0)
    return (random_seed_draw * FEATURE_DEPTH ** (-0.5)).reshape(FEATURE_DEPTH, 4 * FOCUS_COUNT * PER_HEADER_DEPTH).astype(jnp.bfloat16)


def levels(stream_key, extent, shards, smallest, high):
    def one(axis_at, parts):
        heights = jax.random.uniform(jax.random.fold_in(jax.random.fold_in(stream_key, 6), axis_at), (parts,), jnp.float32, smallest / len(shards), high / len(shards))
        return jnp.repeat(jnp.exp(heights), extent[axis_at] // parts).reshape((-1,) + (1,) * (len(extent) - axis_at - 1))

    gain = one(*shards[0])
    for cut in shards[1:]:
        gain = gain * one(*cut)
    return gain


def gaussian(key, dims, scale, bound, cuts=(), kind=jnp.bfloat16):
    gain = levels(key, dims, cuts, -0.22, 0.18) if cuts else 1.0
    result = jax.random.normal(key, dims, jnp.float32) * scale * gain
    return jnp.minimum(jnp.maximum(result, -bound), bound).astype(kind)


def setup_inputs(seed: int = 0, part: int = 0) -> dict:
    arg_keys = jax.random.split(jax.random.key(seed), 15)
    own_keys = jax.random.split(jax.random.fold_in(arg_keys[14], part), 15)
    aligned_chain_features = gaussian(own_keys[0], (GROUPED_CHAINS, WINDOW_SITES_N, FEATURE_DEPTH), 1.0, 6.0, ((1, 128),))
    pair_representation_state = gaussian(own_keys[1], (WINDOW_SITES_N, WINDOW_SITES_N, CZ), 1.0, 6.0, ((0, 128),))
    gap_block_flags = draw_gap_block_flags(jax.random.fold_in(jax.random.fold_in(arg_keys[14], part), 71), part)
    pair_norm_gain = jnp.clip(1.0 + 0.18 * jax.random.normal(arg_keys[3], (CZ,), jnp.float32), 0.1, 1.9)
    pair_head_weight = gaussian(arg_keys[4], (CZ, FOCUS_COUNT), CZ ** -0.5, 0.5)
    horizontal_scaling_factor = jnp.clip(1.0 + 0.18 * jax.random.normal(arg_keys[5], (FEATURE_DEPTH,), jnp.float32), 0.1, 1.9)
    row_input_weight = draw_row_input_weight(jax.random.fold_in(arg_keys[14], 71), part)
    horizontal_final_matrix = gaussian(arg_keys[7], (FOCUS_COUNT * PER_HEADER_DEPTH, FEATURE_DEPTH), (FOCUS_COUNT * PER_HEADER_DEPTH) ** -0.5, 0.375)
    vertical_scaling_factor = jnp.clip(1.0 + 0.18 * jax.random.normal(arg_keys[8], (FEATURE_DEPTH,), jnp.float32), 0.1, 1.9)
    column_input_weight = draw_column_input_weight(jax.random.fold_in(arg_keys[14], 71), part)
    vertical_final_matrix = gaussian(arg_keys[10], (FOCUS_COUNT * PER_HEADER_DEPTH, FEATURE_DEPTH), (FOCUS_COUNT * PER_HEADER_DEPTH) ** -0.5, 0.375)
    feedforward_scaling_factor = jnp.clip(1.0 + 0.18 * jax.random.normal(arg_keys[11], (FEATURE_DEPTH,), jnp.float32), 0.1, 1.9)
    feedforward_widen_matrix = gaussian(arg_keys[12], (FEATURE_DEPTH, WIDENED_UNITS), FEATURE_DEPTH ** -0.5, 0.375)
    feedforward_shrink_matrix = gaussian(arg_keys[13], (WIDENED_UNITS, FEATURE_DEPTH), WIDENED_UNITS ** -0.5, 0.1875)
    return dict(aligned_chain_features=aligned_chain_features, pair_representation_state=pair_representation_state, gap_block_flags=gap_block_flags, pair_norm_gain=pair_norm_gain, pair_head_weight=pair_head_weight, horizontal_scaling_factor=horizontal_scaling_factor, row_input_weight=row_input_weight, horizontal_final_matrix=horizontal_final_matrix, vertical_scaling_factor=vertical_scaling_factor, column_input_weight=column_input_weight, vertical_final_matrix=vertical_final_matrix, feedforward_scaling_factor=feedforward_scaling_factor, feedforward_widen_matrix=feedforward_widen_matrix, feedforward_shrink_matrix=feedforward_shrink_matrix)


EPSILON = 1e-05
MASKED_SCORE = -1000000000.0

def layer_normalize(inputs, scale_gain):
    values_f = inputs.astype(jnp.float32)
    centred = values_f - lax.optimization_barrier(jnp.mean(values_f, axis=-1, keepdims=True))
    spread = lax.optimization_barrier(jnp.mean(centred * centred, axis=-1, keepdims=True))
    return centred * lax.rsqrt(spread + EPSILON) * scale_gain

def project(normed_bf, weights_in):
    projected = jnp.dot(normed_bf, weights_in, preferred_element_type=jnp.float32)
    projected = projected.reshape(projected.shape[0], 4, FOCUS_COUNT, PER_HEADER_DEPTH)
    queries = (projected[:, 0] * PER_HEADER_DEPTH ** (-0.5)).astype(jnp.bfloat16)
    keys_bf = projected[:, 1].astype(jnp.bfloat16)
    values_bf = projected[:, 2].astype(jnp.bfloat16)
    gates = jax.nn.sigmoid(projected[:, 3])
    return (queries, keys_bf, values_bf, gates)

def attend(queries, keys_bf, values_bf, extra, masked):
    scores = jnp.einsum('qhd,khd->hqk', queries.astype(jnp.float32), keys_bf.astype(jnp.float32))
    scores = scores + extra
    scores = jnp.where(masked[None, None, :], MASKED_SCORE, scores)
    weights_bf = jax.nn.softmax(scores, axis=-1).astype(jnp.bfloat16)
    return jnp.einsum('hqk,khd->qhd', weights_bf.astype(jnp.float32), values_bf.astype(jnp.float32))

def reference(aligned_chain_features, pair_representation_state, gap_block_flags, pair_norm_gain, pair_head_weight, horizontal_scaling_factor, row_input_weight, horizontal_final_matrix, vertical_scaling_factor, column_input_weight, vertical_final_matrix, feedforward_scaling_factor, feedforward_widen_matrix, feedforward_shrink_matrix):
    pair_normed = layer_normalize(pair_representation_state, pair_norm_gain).astype(jnp.bfloat16)
    pair_bias = jnp.einsum('ijc,ch->hij', pair_normed.astype(jnp.float32), pair_head_weight.astype(jnp.float32)).astype(jnp.bfloat16)
    bias_f = pair_bias.astype(jnp.float32)
    key_gap_mask = jnp.repeat(gap_block_flags, BLOCK, axis=1)

    def row_attention_update(sequence_entries):
        sequence_rows, gap_keys = sequence_entries
        normed = layer_normalize(sequence_rows, horizontal_scaling_factor).astype(jnp.bfloat16)
        queries, keys_bf, values_bf, gates = project(normed, row_input_weight)
        attended = attend(queries, keys_bf, values_bf, bias_f, gap_keys == 1)
        gated_out = (attended * gates).astype(jnp.bfloat16).reshape(sequence_rows.shape[0], FOCUS_COUNT * PER_HEADER_DEPTH)
        layer_update = jnp.dot(gated_out, horizontal_final_matrix, preferred_element_type=jnp.float32)
        return (sequence_rows.astype(jnp.float32) + layer_update).astype(jnp.bfloat16)
    alignment_first = lax.map(row_attention_update, (aligned_chain_features, key_gap_mask))

    def column_attention_update(res_items):
        res_rows, gap_keys = res_items
        normed = layer_normalize(res_rows, vertical_scaling_factor).astype(jnp.bfloat16)
        queries, keys_bf, values_bf, gates = project(normed, column_input_weight)
        attended = attend(queries, keys_bf, values_bf, jnp.float32(0.0), gap_keys == 1)
        gated_out = (attended * gates).astype(jnp.bfloat16).reshape(res_rows.shape[0], FOCUS_COUNT * PER_HEADER_DEPTH)
        layer_update = jnp.dot(gated_out, vertical_final_matrix, preferred_element_type=jnp.float32)
        return (res_rows.astype(jnp.float32) + layer_update).astype(jnp.bfloat16)
    residue_major = lax.map(column_attention_update, (jnp.transpose(alignment_first, (1, 0, 2)), jnp.transpose(key_gap_mask)))
    alignment_second = jnp.transpose(residue_major, (1, 0, 2))

    def transition_update(sequence_rows):
        normed = layer_normalize(sequence_rows, feedforward_scaling_factor).astype(jnp.bfloat16)
        hidden_bf = jax.nn.relu(jnp.dot(normed, feedforward_widen_matrix, preferred_element_type=jnp.float32)).astype(jnp.bfloat16)
        layer_update = jnp.dot(hidden_bf, feedforward_shrink_matrix, preferred_element_type=jnp.float32)
        return (sequence_rows.astype(jnp.float32) + layer_update).astype(jnp.bfloat16)
    return lax.map(transition_update, alignment_second)
```

```python
import jax
import jax.numpy as jnp
from jax import lax
from jax.experimental import pallas as pl
from jax.experimental.pallas import tpu as pltpu
from jax.sharding import PartitionSpec as P

EPSILON = 1e-05
MASKED_SCORE = -1000000000.0
HEADS = 8
DEPTH = 32
BF = jnp.bfloat16
F32 = jnp.float32
MESH = pl.DeviceIdType.MESH
NT = (((1,), (1,)), ((), ()))


def normalize(values, gain):
    centred = values - jnp.mean(values, axis=-1, keepdims=True)
    spread = jnp.mean(centred * centred, axis=-1, keepdims=True)
    return (centred * lax.rsqrt(spread + EPSILON) * gain).astype(BF)


def mm(a, b):
    return jnp.dot(a, b, preferred_element_type=F32)


def mm_nt(a, b):
    return lax.dot_general(a, b, NT, preferred_element_type=F32)


def selector(source_of, rows):
    o = lax.broadcasted_iota(jnp.int32, (rows, rows), 0)
    i = lax.broadcasted_iota(jnp.int32, (rows, rows), 1)
    return jnp.where(source_of(o) == i, 1.0, 0.0).astype(F32).astype(BF)


def pick(one_hot, rows):
    return mm(one_hot, rows).astype(BF)


def head_lanes(h, rows, width=256):
    lane = lax.broadcasted_iota(jnp.int32, (rows, width), 1)
    return lane // DEPTH == h


def remote(src, dst, send, recv, device):
    return pltpu.make_async_remote_copy(
        src_ref=src,
        dst_ref=dst,
        send_sem=send,
        recv_sem=recv,
        device_id={"res": device},
        device_id_type=MESH,
    )


def row_kernel(
    x_ref, pair_ref, flags_ref, pgain_ref, pw_ref, gain_ref, win_hbm, wout_hbm,
    out_ref,
    win, wout, bloc, xmid, xsend, xrows, bmid, bsend, bias, m1, cmid, csend,
    wsem, xa_s, xa_r, ba_s, ba_r, xb_s, xb_r, bb_s, bb_r, dd_s, dd_r, ca_s, ca_r, cb_s, cb_r,
):
    me = lax.axis_index("res")
    z = me // 16
    k = lax.rem(me, 16)
    y = k // 2
    c = lax.rem(me, 2)
    sib = me + 1 - 2 * c

    load_in = pltpu.make_async_copy(win_hbm, win, wsem.at[0])
    load_out = pltpu.make_async_copy(wout_hbm, wout, wsem.at[1])
    load_in.start()
    load_out.start()

    barrier = pltpu.get_barrier_semaphore()

    def greet(device):
        pl.semaphore_signal(barrier, inc=1, device_id={"res": device}, device_id_type=MESH)

    for j in (4, 3, 5, 2, 6, 1, 7):
        greet(lax.rem(z + j, 8) * 16 + k)
        greet(lax.rem(z + j, 8) * 16 + y * 2 + 1 - c)
    for j in (8, 7, 9, 6, 10, 5, 11, 4, 12, 3, 13, 2, 14, 1, 15):
        greet(z * 16 + lax.rem(k + j, 16))

    normed = normalize(pair_ref[...].astype(F32), pgain_ref[...])
    biases = mm_nt(pw_ref[...], normed).astype(BF)
    bloc[0] = jnp.concatenate([biases[:, 0:128], biases[:, 256:384]], axis=0)
    bloc[1] = jnp.concatenate([biases[:, 128:256], biases[:, 384:512]], axis=0)

    pl.semaphore_wait(barrier, 29)

    for j in (8, 7, 9, 6, 10, 5, 11, 4, 12, 3, 13, 2, 14, 1, 15):
        kp = lax.rem(k + j, 16)
        remote(x_ref.at[kp], xmid.at[k], xa_s, xa_r, z * 16 + kp).start()
    xmid[k] = x_ref[k]
    for j in (4, 3, 5, 2, 6, 1, 7):
        yp = lax.rem(y + j, 8)
        remote(bloc.at[0], bmid.at[k], ba_s, ba_r, z * 16 + yp * 2).start()
        zp = lax.rem(z + j, 8)
        remote(bloc.at[1], bmid.at[z * 2 + c], ba_s, ba_r, zp * 16 + y * 2 + 1).start()

    @pl.when(c == 0)
    def _():
        remote(bloc.at[1], bmid.at[z * 2], ba_s, ba_r, sib).start()
        bmid[k] = bloc[0]

    @pl.when(c == 1)
    def _():
        remote(bloc.at[0], bmid.at[k], ba_s, ba_r, sib).start()
        bmid[z * 2 + 1] = bloc[1]

    by_z = selector(lambda o: lax.rem(o, 32) // 2 * 16 + o // 32 * 2 + lax.rem(o, 2), 256)
    by_h = selector(lambda o: lax.rem(o, 32) // 2 * 16 + lax.rem(o, 2) * 8 + o // 32, 256)
    by_k = selector(lambda o: lax.rem(o, 16) // 2 * 32 + o // 16 * 2 + lax.rem(o, 2), 256)
    natural = selector(lambda o: lax.rem(o, 32) // 4 * 32 + o // 32 * 4 + lax.rem(o, 4), 256)

    remote(xmid.at[pl.ds(0, 15)], xmid.at[pl.ds(0, 15)], xa_s, xa_r, sib).wait_recv()
    xsend[...] = pick(by_z, xmid[...].reshape(256, 256)).reshape(8, 32, 256)
    for j in (4, 3, 5, 2, 6, 1, 7):
        zp = lax.rem(z + j, 8)
        remote(xsend.at[zp], xrows.at[z], xb_s, xb_r, zp * 16 + k).start()
    xrows[z] = xsend[z]

    remote(bmid.at[pl.ds(0, 15)], bmid.at[pl.ds(0, 15)], ba_s, ba_r, sib).wait_recv()
    bsend[...] = pick(by_h, bmid[...].reshape(256, 128)).reshape(8, 32, 128)
    place = pl.multiple_of(jnp.where(c == 0, z, y) * 32, 32)
    for g in range(4):
        for j in (4, 3, 5, 2, 6, 1, 7):
            peer = jnp.where(
                c == 0, lax.rem(z + j, 8) * 16 + k, z * 16 + lax.rem(y + j, 8) * 2 + c
            )
            remote(
                bsend.at[pl.ds(2 * g, 2)],
                bias.at[c, pl.ds(2 * g, 2), pl.ds(place, 32)],
                bb_s.at[g],
                bb_r.at[g],
                peer,
            ).start()
    bias[c, :, pl.ds(place, 32), :] = bsend[...]

    def arrived(g):
        part = bias.at[0, pl.ds(2 * g, 2), pl.ds(0, 224)]
        remote(part, part, bb_s.at[g], bb_r.at[g], sib).wait_recv()
        part = bias.at[c, pl.ds(2 * g, 2)]
        remote(part, part, dd_s.at[g], dd_r.at[g], sib).start()

    def complete(g):
        part = bias.at[c, pl.ds(2 * g, 2)]
        remote(part, part, dd_s.at[g], dd_r.at[g], sib).wait_recv()

    seq = lax.broadcasted_iota(jnp.int32, (2, 128), 1)
    gaps = jnp.sum(jnp.where(seq == 8 * k + z, flags_ref[...], 0), axis=1, keepdims=True)
    half = lax.broadcasted_iota(jnp.int32, (1, 256), 1) // 128
    masked = jnp.where(half == 0, gaps[0:1], gaps[1:2]) == 1

    load_in.wait()
    load_out.wait()
    remote(xrows.at[pl.ds(0, 7)], xrows.at[pl.ds(0, 7)], xb_s, xb_r, sib).wait_recv()
    rows_bf = xrows[...].reshape(256, 256)
    rows = rows_bf.astype(F32)
    row_normed = normalize(rows, gain_ref[...])
    queries = (mm(row_normed, win[:, 0:256]) * DEPTH ** (-0.5)).astype(BF)
    keys = mm(row_normed, win[:, 256:512]).astype(BF)
    values = mm(row_normed, win[:, 512:768]).astype(BF)
    gates = jax.nn.sigmoid(mm(row_normed, win[:, 768:1024]))

    arrived(0)
    arrived(1)
    total = jnp.zeros((256, 512), F32)
    for g in range(4):
        complete(g)
        exps = []
        weights = []
        for h in (2 * g, 2 * g + 1):
            mine = head_lanes(h, 256)
            scores = mm_nt(jnp.where(mine, queries, 0), keys)
            added = jnp.concatenate(
                [bias[0, h].astype(F32), mm(natural, bias[1, h])], axis=1
            )
            scores = jnp.where(masked, MASKED_SCORE, scores + added)
            scores = scores - jnp.max(scores, axis=1, keepdims=True)
            exps.append(jnp.exp(scores).astype(BF))
            weights.append(
                jnp.concatenate(
                    [jnp.where(mine, values, 0), jnp.where(mine, 1.0, 0.0).astype(BF)], axis=1
                )
            )
        total = total + mm(jnp.concatenate(exps, axis=1), jnp.concatenate(weights, axis=0))
        if g + 2 < 4:
            arrived(g + 2)
    gated = (total[:, 0:256] / total[:, 256:512] * gates).astype(BF)
    m1[...] = (rows + mm(gated, wout[...])).astype(BF).reshape(8, 32, 256)

    for j in (4, 3, 5, 2, 6, 1, 7):
        zp = lax.rem(z + j, 8)
        remote(m1.at[zp], cmid.at[z], ca_s, ca_r, zp * 16 + k).start()
    cmid[z] = m1[z]
    remote(cmid.at[pl.ds(0, 7)], cmid.at[pl.ds(0, 7)], ca_s, ca_r, sib).wait_recv()
    csend[...] = pick(by_k, cmid[...].reshape(256, 256)).reshape(16, 16, 256)
    for j in (8, 7, 9, 6, 10, 5, 11, 4, 12, 3, 13, 2, 14, 1, 15):
        kp = lax.rem(k + j, 16)
        remote(csend.at[kp], out_ref.at[k], cb_s, cb_r, z * 16 + kp).start()
    out_ref[k] = csend[k]
    remote(csend.at[pl.ds(0, 15)], csend.at[pl.ds(0, 15)], cb_s, cb_r, sib).wait_recv()

    remote(xmid.at[pl.ds(0, 15)], xmid.at[pl.ds(0, 15)], xa_s, xa_r, sib).wait_send()
    remote(bmid.at[pl.ds(0, 15)], bmid.at[pl.ds(0, 15)], ba_s, ba_r, sib).wait_send()
    remote(xrows.at[pl.ds(0, 7)], xrows.at[pl.ds(0, 7)], xb_s, xb_r, sib).wait_send()
    for g in range(4):
        part = bias.at[0, pl.ds(2 * g, 2), pl.ds(0, 224)]
        remote(part, part, bb_s.at[g], bb_r.at[g], sib).wait_send()
        part = bias.at[c, pl.ds(2 * g, 2)]
        remote(part, part, dd_s.at[g], dd_r.at[g], sib).wait_send()
    remote(cmid.at[pl.ds(0, 7)], cmid.at[pl.ds(0, 7)], ca_s, ca_r, sib).wait_send()
    remote(csend.at[pl.ds(0, 15)], csend.at[pl.ds(0, 15)], cb_s, cb_r, sib).wait_send()


def column_kernel(
    m_ref, flags_ref, gain_ref, win_ref, wout_ref, tgain_ref, wide_ref, shrink_ref, out_ref
):
    z = lax.axis_index("res") // 16
    apart = selector(lambda o: lax.rem(o, 128) * 2 + o // 128, 256)
    together = selector(lambda o: lax.rem(o, 2) * 128 + o // 2, 256)
    first = mm(apart, m_ref[...])
    normed = normalize(first, gain_ref[...])
    queries = (mm(normed, win_ref[:, 0:256]) * DEPTH ** (-0.5)).astype(BF)
    keys = mm(normed, win_ref[:, 256:512]).astype(BF)
    values = mm(normed, win_ref[:, 512:768]).astype(BF)
    gates = jax.nn.sigmoid(mm(normed, win_ref[:, 768:1024]))
    masked = jnp.where(z // 4 == 0, flags_ref[0:1, :], flags_ref[1:2, :]) == 1
    attended = []
    for r in range(2):
        q, t, v = (a[128 * r : 128 * r + 128] for a in (queries, keys, values))
        exps = []
        weights = []
        for h in range(HEADS):
            mine = head_lanes(h, 128)
            scores = mm_nt(jnp.where(mine, q, 0), t)
            scores = jnp.where(masked, MASKED_SCORE, scores)
            scores = scores - jnp.max(scores, axis=1, keepdims=True)
            exps.append(jnp.exp(scores).astype(BF))
            weights.append(
                jnp.concatenate(
                    [jnp.where(mine, v, 0), jnp.where(mine, 1.0, 0.0).astype(BF)], axis=1
                )
            )
        total = mm(jnp.concatenate(exps, axis=1), jnp.concatenate(weights, axis=0))
        attended.append(total[:, 0:256] / total[:, 256:512])
    gated = (jnp.concatenate(attended, axis=0) * gates).astype(BF)
    second = (first + mm(gated, wout_ref[...])).astype(BF)
    second_f = second.astype(F32)
    hidden = jnp.maximum(mm(normalize(second_f, tgain_ref[...]), wide_ref[...]), 0.0).astype(BF)
    result = (second_f + mm(hidden, shrink_ref[...])).astype(BF)
    out_ref[...] = pick(together, result)


def body(
    aligned_chain_features,
    pair_representation_state,
    gap_block_flags,
    pair_norm_gain,
    pair_head_weight,
    horizontal_scaling_factor,
    row_input_weight,
    horizontal_final_matrix,
    vertical_scaling_factor,
    column_input_weight,
    vertical_final_matrix,
    feedforward_scaling_factor,
    feedforward_widen_matrix,
    feedforward_shrink_matrix,
):
    vmem = pl.BlockSpec(memory_space=pltpu.VMEM)
    hbm = pl.BlockSpec(memory_space=pl.ANY)
    dma = pltpu.SemaphoreType.DMA
    flags = jnp.transpose(gap_block_flags)
    first = pl.pallas_call(
        row_kernel,
        out_shape=jax.ShapeDtypeStruct((16, 16, 256), BF),
        in_specs=[vmem] * 6 + [hbm] * 2,
        out_specs=vmem,
        scratch_shapes=[
            pltpu.VMEM((256, 1024), BF),
            pltpu.VMEM((256, 256), BF),
            pltpu.VMEM((2, 16, 128), BF),
            pltpu.VMEM((16, 16, 256), BF),
            pltpu.VMEM((8, 32, 256), BF),
            pltpu.VMEM((8, 32, 256), BF),
            pltpu.VMEM((16, 16, 128), BF),
            pltpu.VMEM((8, 32, 128), BF),
            pltpu.VMEM((2, 8, 256, 128), BF),
            pltpu.VMEM((8, 32, 256), BF),
            pltpu.VMEM((8, 32, 256), BF),
            pltpu.VMEM((16, 16, 256), BF),
            dma((2,)), dma, dma, dma, dma, dma, dma,
            dma((4,)), dma((4,)), dma((4,)), dma((4,)), dma, dma, dma, dma,
        ],
        name="row_attention",
        compiler_params=pltpu.CompilerParams(
            collective_id=0, has_side_effects=True, vmem_limit_bytes=40 << 20
        ),
    )(
        aligned_chain_features.reshape(16, 16, 256),
        pair_representation_state.reshape(512, 128),
        flags,
        pair_norm_gain.reshape(1, 128),
        jnp.transpose(pair_head_weight),
        horizontal_scaling_factor.reshape(1, 256),
        row_input_weight,
        horizontal_final_matrix,
    )
    result = pl.pallas_call(
        column_kernel,
        out_shape=jax.ShapeDtypeStruct((256, 256), BF),
        in_specs=[vmem] * 8,
        out_specs=vmem,
        name="column_attention",
        compiler_params=pltpu.CompilerParams(vmem_limit_bytes=40 << 20),
    )(
        first.reshape(256, 256),
        flags,
        vertical_scaling_factor.reshape(1, 256),
        column_input_weight,
        vertical_final_matrix,
        feedforward_scaling_factor.reshape(1, 256),
        feedforward_widen_matrix,
        feedforward_shrink_matrix,
    )
    return result.reshape(128, 2, 256)


def solution(mesh):
    placed = (
        P("dp", "res", None),
        P(("dp", "res"), None, None),
        P("dp", None),
        P(),
        P(),
        P(),
        P(),
        P(),
        P(),
        P(),
        P(),
        P(),
        P(),
        P(),
    )
    return jax.shard_map(
        body, mesh=mesh, in_specs=placed, out_specs=P("dp", "res", None), check_vma=False
    )
```

```python
import jax
import jax.numpy as jnp
from jax import lax
from jax.experimental import pallas as pl
from jax.experimental.pallas import tpu as pltpu
from jax.sharding import PartitionSpec as P

EPSILON = 1e-05
MASKED_SCORE = -1000000000.0
HEADS = 8
DEPTH = 32
BF = jnp.bfloat16
F32 = jnp.float32
MESH = pl.DeviceIdType.MESH
NT = (((1,), (1,)), ((), ()))
FAR_Z = (4, 3, 5, 2, 6, 1, 7)
FAR_K = (8, 7, 9, 6, 10, 5, 11, 4, 12, 3, 13, 2, 14, 1, 15)


def normalize(values, gain):
    centred = values - jnp.mean(values, axis=-1, keepdims=True)
    spread = jnp.mean(centred * centred, axis=-1, keepdims=True)
    return (centred * lax.rsqrt(spread + EPSILON) * gain).astype(BF)


def mm(a, b):
    return jnp.dot(a, b, preferred_element_type=F32)


def mm_nt(a, b):
    return lax.dot_general(a, b, NT, preferred_element_type=F32)


def selector(source_of, rows):
    o = lax.broadcasted_iota(jnp.int32, (rows, rows), 0)
    i = lax.broadcasted_iota(jnp.int32, (rows, rows), 1)
    return jnp.where(source_of(o) == i, 1.0, 0.0).astype(F32).astype(BF)


def pick(one_hot, rows):
    return mm(one_hot, rows).astype(BF)


def head_lanes(h, rows, width=256):
    lane = lax.broadcasted_iota(jnp.int32, (rows, width), 1)
    return lane // DEPTH == h


def value_and_count(mine, values):
    count = jnp.where(mine, 1.0, 0.0).astype(BF)
    return jnp.concatenate([jnp.where(mine, values, 0), count], axis=1)


def remote(src, dst, send, recv, device):
    return pltpu.make_async_remote_copy(
        src_ref=src,
        dst_ref=dst,
        send_sem=send,
        recv_sem=recv,
        device_id={"res": device},
        device_id_type=MESH,
    )


def kernel(
    x_hbm, pair_hbm, flags_hbm, pgain_hbm, pw_hbm, rgain_hbm, rin_hbm, rout_hbm,
    cgain_hbm, cin_hbm, cout_hbm, tgain_hbm, wide_hbm, shrink_hbm,
    out_ref,
    pair, flags, pgain, pw, rgain, rin, rout, cgain, cin, cout, tgain, wide, shrink,
    bloc, xmid, xsend, xrows, bmid, bsend, bias, m1, cmid, csend, cols,
    load_sem, own_sem, xa_s, xa_r, ba_s, ba_r, xb_s, xb_r,
    bb_s, bb_r, dd_s, dd_r, ca_s, ca_r, cb_s, cb_r,
):
    me = lax.axis_index("res")
    z = me // 16
    k = lax.rem(me, 16)
    y = k // 2
    c = lax.rem(me, 2)
    sib = me + 1 - 2 * c

    barrier = pltpu.get_barrier_semaphore()

    def greet(device):
        pl.semaphore_signal(barrier, inc=1, device_id={"res": device}, device_id_type=MESH)

    for j in FAR_Z:
        greet(lax.rem(z + j, 8) * 16 + k)
        greet(lax.rem(z + j, 8) * 16 + y * 2 + 1 - c)
    for j in FAR_K:
        greet(z * 16 + lax.rem(k + j, 16))

    loads = [
        pltpu.make_async_copy(source, target, load_sem.at[n])
        for n, (source, target) in enumerate((
            (pair_hbm, pair), (pgain_hbm, pgain), (pw_hbm, pw), (flags_hbm, flags),
            (rgain_hbm, rgain), (rin_hbm, rin), (rout_hbm, rout),
            (cgain_hbm, cgain), (cin_hbm, cin), (cout_hbm, cout),
            (tgain_hbm, tgain), (wide_hbm, wide), (shrink_hbm, shrink),
        ))
    ]
    for load in loads:
        load.start()
    own = pltpu.make_async_copy(
        x_hbm.at[pl.ds(8 * k, 8)], xmid.at[pl.ds(8 * k, 8)], own_sem
    )
    own.start()

    for load in loads[0:3]:
        load.wait()
    normed = normalize(pair[...].astype(F32), pgain[...])
    biases = mm_nt(pw[...], normed).astype(BF)
    bloc[0] = jnp.concatenate([biases[:, 0:128], biases[:, 256:384]], axis=0)
    bloc[1] = jnp.concatenate([biases[:, 128:256], biases[:, 384:512]], axis=0)

    pl.semaphore_wait(barrier, 29)

    for j in FAR_K:
        kp = lax.rem(k + j, 16)
        remote(
            x_hbm.at[pl.ds(8 * kp, 8)], xmid.at[pl.ds(8 * k, 8)], xa_s, xa_r, z * 16 + kp
        ).start()
    for j in FAR_Z:
        yp = lax.rem(y + j, 8)
        remote(bloc.at[0], bmid.at[k], ba_s, ba_r, z * 16 + yp * 2).start()
        zp = lax.rem(z + j, 8)
        remote(bloc.at[1], bmid.at[z * 2 + c], ba_s, ba_r, zp * 16 + y * 2 + 1).start()

    @pl.when(c == 0)
    def _():
        remote(bloc.at[1], bmid.at[z * 2], ba_s, ba_r, sib).start()
        bmid[k] = bloc[0]

    @pl.when(c == 1)
    def _():
        remote(bloc.at[0], bmid.at[k], ba_s, ba_r, sib).start()
        bmid[z * 2 + 1] = bloc[1]

    by_z = selector(lambda o: lax.rem(o, 32) // 2 * 16 + o // 32 * 2 + lax.rem(o, 2), 256)
    by_h = selector(lambda o: lax.rem(o, 32) // 2 * 16 + lax.rem(o, 2) * 8 + o // 32, 256)
    natural = selector(lambda o: lax.rem(o, 32) // 4 * 32 + o // 32 * 4 + lax.rem(o, 4), 256)

    own.wait()
    remote(xmid.at[pl.ds(0, 120)], xmid.at[pl.ds(0, 120)], xa_s, xa_r, sib).wait_recv()
    xsend[...] = pick(by_z, xmid[...].reshape(256, 256)).reshape(8, 32, 256)
    for j in FAR_Z:
        zp = lax.rem(z + j, 8)
        remote(xsend.at[zp], xrows.at[z], xb_s, xb_r, zp * 16 + k).start()
    xrows[z] = xsend[z]

    remote(bmid.at[pl.ds(0, 15)], bmid.at[pl.ds(0, 15)], ba_s, ba_r, sib).wait_recv()
    bsend[...] = pick(by_h, bmid[...].reshape(256, 128)).reshape(8, 32, 128)
    place = pl.multiple_of(jnp.where(c == 0, z, y) * 32, 32)
    for g in range(4):
        for j in FAR_Z:
            peer = jnp.where(
                c == 0, lax.rem(z + j, 8) * 16 + k, z * 16 + lax.rem(y + j, 8) * 2 + c
            )
            remote(
                bsend.at[pl.ds(2 * g, 2)],
                bias.at[c, pl.ds(2 * g, 2), pl.ds(place, 32)],
                bb_s.at[g],
                bb_r.at[g],
                peer,
            ).start()
    bias[c, :, pl.ds(place, 32), :] = bsend[...]

    def arrived(g):
        part = bias.at[0, pl.ds(2 * g, 2), pl.ds(0, 224)]
        remote(part, part, bb_s.at[g], bb_r.at[g], sib).wait_recv()
        part = bias.at[c, pl.ds(2 * g, 2)]
        remote(part, part, dd_s.at[g], dd_r.at[g], sib).start()

    def complete(g):
        part = bias.at[c, pl.ds(2 * g, 2)]
        remote(part, part, dd_s.at[g], dd_r.at[g], sib).wait_recv()

    for load in loads[3:]:
        load.wait()
    seq = lax.broadcasted_iota(jnp.int32, (2, 128), 1)
    gaps = jnp.sum(jnp.where(seq == 8 * k + z, flags[...], 0), axis=1, keepdims=True)
    half = lax.broadcasted_iota(jnp.int32, (1, 256), 1) // 128
    masked = jnp.where(half == 0, gaps[0:1], gaps[1:2]) == 1

    remote(xrows.at[pl.ds(0, 7)], xrows.at[pl.ds(0, 7)], xb_s, xb_r, sib).wait_recv()
    rows = xrows[...].reshape(256, 256).astype(F32)
    row_normed = normalize(rows, rgain[...])
    queries = (mm(row_normed, rin[:, 0:256]) * DEPTH ** (-0.5)).astype(BF)
    keys = mm(row_normed, rin[:, 256:512]).astype(BF)
    values = mm(row_normed, rin[:, 512:768]).astype(BF)
    gates = jax.nn.sigmoid(mm(row_normed, rin[:, 768:1024]))

    arrived(0)
    arrived(1)
    total = jnp.zeros((256, 512), F32)
    for g in range(4):
        complete(g)
        exps = []
        weights = []
        for h in (2 * g, 2 * g + 1):
            mine = head_lanes(h, 256)
            scores = mm_nt(jnp.where(mine, queries, 0), keys)
            added = jnp.concatenate(
                [bias[0, h].astype(F32), mm(natural, bias[1, h])], axis=1
            )
            scores = jnp.where(masked, MASKED_SCORE, scores + added)
            scores = scores - jnp.max(scores, axis=1, keepdims=True)
            exps.append(jnp.exp(scores).astype(BF))
            weights.append(value_and_count(mine, values))
        total = total + mm(jnp.concatenate(exps, axis=1), jnp.concatenate(weights, axis=0))
        if g + 2 < 4:
            arrived(g + 2)
    gated = (total[:, 0:256] / total[:, 256:512] * gates).astype(BF)
    m1[...] = (rows + mm(gated, rout[...])).astype(BF).reshape(8, 32, 256)

    for j in FAR_Z:
        zp = lax.rem(z + j, 8)
        remote(m1.at[zp], cmid.at[z], ca_s, ca_r, zp * 16 + k).start()
    cmid[z] = m1[z]
    by_k = selector(lambda o: lax.rem(o, 16) // 2 * 32 + o // 16 * 2 + lax.rem(o, 2), 256)
    apart = selector(lambda o: lax.rem(o, 128) * 2 + o // 128, 256)
    together = selector(lambda o: lax.rem(o, 2) * 128 + o // 2, 256)
    masked = jnp.where(z // 4 == 0, flags[0:1, :], flags[1:2, :]) == 1
    remote(cmid.at[pl.ds(0, 7)], cmid.at[pl.ds(0, 7)], ca_s, ca_r, sib).wait_recv()
    csend[...] = pick(by_k, cmid[...].reshape(256, 256)).reshape(16, 16, 256)
    for j in FAR_K:
        kp = lax.rem(k + j, 16)
        remote(csend.at[kp], cols.at[k], cb_s, cb_r, z * 16 + kp).start()
    cols[k] = csend[k]
    remote(csend.at[pl.ds(0, 15)], csend.at[pl.ds(0, 15)], cb_s, cb_r, sib).wait_recv()

    first = mm(apart, cols[...].reshape(256, 256))
    normed = normalize(first, cgain[...])
    queries = (mm(normed, cin[:, 0:256]) * DEPTH ** (-0.5)).astype(BF)
    keys = mm(normed, cin[:, 256:512]).astype(BF)
    values = mm(normed, cin[:, 512:768]).astype(BF)
    gates = jax.nn.sigmoid(mm(normed, cin[:, 768:1024]))
    attended = []
    for r in range(2):
        q, t, v = (a[128 * r : 128 * r + 128] for a in (queries, keys, values))
        exps = []
        weights = []
        for h in range(HEADS):
            mine = head_lanes(h, 128)
            scores = mm_nt(jnp.where(mine, q, 0), t)
            scores = jnp.where(masked, MASKED_SCORE, scores)
            scores = scores - jnp.max(scores, axis=1, keepdims=True)
            exps.append(jnp.exp(scores).astype(BF))
            weights.append(value_and_count(mine, v))
        total = mm(jnp.concatenate(exps, axis=1), jnp.concatenate(weights, axis=0))
        attended.append(total[:, 0:256] / total[:, 256:512])
    gated = (jnp.concatenate(attended, axis=0) * gates).astype(BF)
    second = (first + mm(gated, cout[...])).astype(BF).astype(F32)
    hidden = jnp.maximum(mm(normalize(second, tgain[...]), wide[...]), 0.0).astype(BF)
    result = (second + mm(hidden, shrink[...])).astype(BF)
    out_ref[...] = pick(together, result).reshape(128, 2, 256)

    remote(xmid.at[pl.ds(0, 120)], xmid.at[pl.ds(0, 120)], xa_s, xa_r, sib).wait_send()
    remote(bmid.at[pl.ds(0, 15)], bmid.at[pl.ds(0, 15)], ba_s, ba_r, sib).wait_send()
    remote(xrows.at[pl.ds(0, 7)], xrows.at[pl.ds(0, 7)], xb_s, xb_r, sib).wait_send()
    for g in range(4):
        part = bias.at[0, pl.ds(2 * g, 2), pl.ds(0, 224)]
        remote(part, part, bb_s.at[g], bb_r.at[g], sib).wait_send()
        part = bias.at[c, pl.ds(2 * g, 2)]
        remote(part, part, dd_s.at[g], dd_r.at[g], sib).wait_send()
    remote(cmid.at[pl.ds(0, 7)], cmid.at[pl.ds(0, 7)], ca_s, ca_r, sib).wait_send()
    remote(csend.at[pl.ds(0, 15)], csend.at[pl.ds(0, 15)], cb_s, cb_r, sib).wait_send()


def body(
    aligned_chain_features,
    pair_representation_state,
    gap_block_flags,
    pair_norm_gain,
    pair_head_weight,
    horizontal_scaling_factor,
    row_input_weight,
    horizontal_final_matrix,
    vertical_scaling_factor,
    column_input_weight,
    vertical_final_matrix,
    feedforward_scaling_factor,
    feedforward_widen_matrix,
    feedforward_shrink_matrix,
):
    dma = pltpu.SemaphoreType.DMA
    operands = (
        aligned_chain_features,
        pair_representation_state.reshape(512, 128),
        jnp.transpose(gap_block_flags),
        pair_norm_gain.reshape(1, 128),
        jnp.transpose(pair_head_weight),
        horizontal_scaling_factor.reshape(1, 256),
        row_input_weight,
        horizontal_final_matrix,
        vertical_scaling_factor.reshape(1, 256),
        column_input_weight,
        vertical_final_matrix,
        feedforward_scaling_factor.reshape(1, 256),
        feedforward_widen_matrix,
        feedforward_shrink_matrix,
    )
    return pl.pallas_call(
        kernel,
        out_shape=jax.ShapeDtypeStruct((128, 2, 256), BF),
        in_specs=[pl.BlockSpec(memory_space=pl.ANY)] * len(operands),
        out_specs=pl.BlockSpec(memory_space=pltpu.VMEM),
        scratch_shapes=[pltpu.VMEM(a.shape, a.dtype) for a in operands[1:]]
        + [
            pltpu.VMEM((2, 16, 128), BF),
            pltpu.VMEM((128, 2, 256), BF),
            pltpu.VMEM((8, 32, 256), BF),
            pltpu.VMEM((8, 32, 256), BF),
            pltpu.VMEM((16, 16, 128), BF),
            pltpu.VMEM((8, 32, 128), BF),
            pltpu.VMEM((2, 8, 256, 128), BF),
            pltpu.VMEM((8, 32, 256), BF),
            pltpu.VMEM((8, 32, 256), BF),
            pltpu.VMEM((16, 16, 256), BF),
            pltpu.VMEM((16, 16, 256), BF),
            dma((13,)), dma, dma, dma, dma, dma, dma, dma,
            dma((4,)), dma((4,)), dma((4,)), dma((4,)), dma, dma, dma, dma,
        ],
        name="evoformer",
        compiler_params=pltpu.CompilerParams(
            collective_id=0, has_side_effects=True, vmem_limit_bytes=56 << 20
        ),
    )(*operands)


def solution(mesh):
    placed = (
        P("dp", "res", None),
        P(("dp", "res"), None, None),
        P("dp", None),
        P(),
        P(),
        P(),
        P(),
        P(),
        P(),
        P(),
        P(),
        P(),
        P(),
        P(),
    )
    return jax.shard_map(
        body, mesh=mesh, in_specs=placed, out_specs=P("dp", "res", None), check_vma=False
    )
```

```python
import jax
import jax.numpy as jnp
from jax import lax
from jax.experimental import pallas as pl
from jax.experimental.pallas import tpu as pltpu
from jax.sharding import PartitionSpec as P

EPSILON = 1e-05
MASKED_SCORE = -1000000000.0
HEADS = 8
DEPTH = 32
BF = jnp.bfloat16
F32 = jnp.float32
MESH = pl.DeviceIdType.MESH
NT = (((1,), (1,)), ((), ()))
FAR_Z = (4, 3, 5, 2, 6, 1, 7)
FAR = sorted(
    [(dz, dy, dc) for dz in range(8) for dy in range(8) for dc in range(2)][1:],
    key=lambda d: -min(d[0], 8 - d[0]) - min(d[1], 8 - d[1]),
)
FAR_K = (8, 7, 9, 6, 10, 5, 11, 4, 12, 3, 13, 2, 14, 1, 15)


def normalize(values, gain):
    centred = values - jnp.mean(values, axis=-1, keepdims=True)
    spread = jnp.mean(centred * centred, axis=-1, keepdims=True)
    return (centred * lax.rsqrt(spread + EPSILON) * gain).astype(BF)


def mm(a, b):
    return jnp.dot(a, b, preferred_element_type=F32)


def mm_nt(a, b):
    return lax.dot_general(a, b, NT, preferred_element_type=F32)


def selector(source_of, rows):
    o = lax.broadcasted_iota(jnp.int32, (rows, rows), 0)
    i = lax.broadcasted_iota(jnp.int32, (rows, rows), 1)
    return jnp.where(source_of(o) == i, 1.0, 0.0).astype(F32).astype(BF)


def pick(one_hot, rows):
    return mm(one_hot, rows).astype(BF)


def head_lanes(h, rows, width=128):
    lane = lax.broadcasted_iota(jnp.int32, (rows, width), 1)
    return lane // DEPTH == h


def value_and_count(mine, values):
    count = jnp.where(mine, 1.0, 0.0).astype(BF)
    return jnp.concatenate([jnp.where(mine, values, 0), count], axis=1)


def remote(src, dst, send, recv, device):
    return pltpu.make_async_remote_copy(
        src_ref=src,
        dst_ref=dst,
        send_sem=send,
        recv_sem=recv,
        device_id={"res": device},
        device_id_type=MESH,
    )


def kernel(
    x_hbm, pair_hbm, flags_hbm, pgain_hbm, pw_hbm, rgain_hbm, rin_hbm, rout_hbm,
    cgain_hbm, cin_hbm, cout_hbm, tgain_hbm, wide_hbm, shrink_hbm,
    out_ref,
    pair, flags, pgain, pw, rgain, rin, rout, cgain, cin, cout, tgain, wide, shrink,
    bloc, bmid, bsend, bias, xloc, xmid, xsend, xrows, gsend, cols,
    load_sem, rin_sem, own_sem, ba_s, ba_r, bb_s, bb_r, xa_s, xa_r, xb_s, xb_r,
    xd_s, xd_r, g_s, g_r,
):
    me = lax.axis_index("res")
    z = me // 16
    k = lax.rem(me, 16)
    y = k // 2
    c = lax.rem(me, 2)
    sib = me + 1 - 2 * c

    barrier = pltpu.get_barrier_semaphore()

    def greet(device):
        pl.semaphore_signal(barrier, inc=1, device_id={"res": device}, device_id_type=MESH)

    for j in FAR_Z:
        greet(lax.rem(z + j, 8) * 16 + k)
        greet(lax.rem(z + j, 8) * 16 + y * 2 + 1 - c)
    for j in FAR_K:
        greet(z * 16 + lax.rem(k + j, 16))

    loads = [
        pltpu.make_async_copy(source, target, load_sem.at[n])
        for n, (source, target) in enumerate((
            (pair_hbm, pair), (pgain_hbm, pgain), (pw_hbm, pw), (flags_hbm, flags),
            (rgain_hbm, rgain), (rout_hbm, rout),
            (cgain_hbm, cgain), (cin_hbm, cin), (cout_hbm, cout),
            (tgain_hbm, tgain), (wide_hbm, wide), (shrink_hbm, shrink), (x_hbm, xloc),
        ))
    ]
    loads += [
        pltpu.make_async_copy(
            rin_hbm.at[:, pl.ds(pl.multiple_of(t * 256 + c * 128, 128), 128)],
            rin.at[t],
            rin_sem.at[t],
        )
        for t in range(4)
    ]
    for load in loads:
        load.start()
    own = pltpu.make_async_copy(
        x_hbm.at[pl.ds(8 * k, 8)], xmid.at[pl.ds(8 * k, 8)], own_sem.at[0]
    )
    own.start()

    for load in loads[0:3]:
        load.wait()
    normed = normalize(pair[...].astype(F32), pgain[...])
    biases = mm_nt(pw[...], normed)
    for group in range(2):
        heads = biases[4 * group : 4 * group + 4]
        bloc[group] = jnp.concatenate(
            [heads[:, 128 * n : 128 * n + 128] for n in range(4)], axis=0
        ).astype(BF)

    pl.semaphore_wait(barrier, 29)

    for j in FAR_Z:
        yp = lax.rem(y + j, 8)
        remote(bloc.at[0], bmid.at[k], ba_s, ba_r, z * 16 + yp * 2).start()
        zp = lax.rem(z + j, 8)
        remote(bloc.at[1], bmid.at[z * 2 + c], ba_s, ba_r, zp * 16 + y * 2 + 1).start()

    @pl.when(c == 0)
    def _():
        remote(bloc.at[1], bmid.at[z * 2], ba_s, ba_r, sib).start()
        bmid[k] = bloc[0]

    @pl.when(c == 1)
    def _():
        remote(bloc.at[0], bmid.at[k], ba_s, ba_r, sib).start()
        bmid[z * 2 + 1] = bloc[1]

    for j in FAR_K:
        kp = lax.rem(k + j, 16)
        remote(
            x_hbm.at[pl.ds(8 * kp, 8)], xmid.at[pl.ds(8 * k, 8)], xa_s, xa_r, z * 16 + kp
        ).start()

    by_h = selector(
        lambda o: lax.rem(o, 32) // 2 * 16 + lax.rem(o, 2) * 8 + o // 128 * 4
        + lax.rem(o, 128) // 32,
        256,
    )
    by_z = selector(lambda o: lax.rem(o, 32) // 2 * 16 + o // 32 * 2 + lax.rem(o, 2), 256)
    natural = selector(
        lambda o: jnp.where(c == 0, o, lax.rem(o, 32) // 4 * 32 + o // 32 * 4 + lax.rem(o, 4)),
        256,
    )

    def spread(g):
        for j in FAR_Z:
            peer = jnp.where(
                c == 0, lax.rem(z + j, 8) * 16 + k, z * 16 + lax.rem(y + j, 8) * 2 + c
            )
            remote(
                bsend.at[g], bias.at[g, pl.ds(place, 32)], bb_s.at[g], bb_r.at[g], peer
            ).start()

    place = pl.multiple_of(jnp.where(c == 0, z, y) * 32, 32)
    remote(bmid.at[pl.ds(0, 15)], bmid.at[pl.ds(0, 15)], ba_s, ba_r, sib).wait_recv()
    sorted_bias = pick(by_h, bmid[...].reshape(256, 128))
    bsend[...] = jnp.concatenate([sorted_bias[0:128], sorted_bias[128:256]], axis=1).reshape(
        4, 32, 256
    )
    spread(0)

    own.wait()
    remote(xmid.at[pl.ds(0, 120)], xmid.at[pl.ds(0, 120)], xa_s, xa_r, sib).wait_recv()
    xsend[...] = pick(by_z, xmid[...].reshape(256, 256)).reshape(8, 32, 256)
    for j in FAR_Z:
        zp = lax.rem(z + j, 8)
        remote(xsend.at[zp], xrows.at[c, z], xb_s, xb_r, zp * 16 + k).start()
    xrows[c, z] = xsend[z]
    for g in range(1, 4):
        spread(g)
    bias[:, pl.ds(place, 32), :] = bsend[...]

    for load in loads[3:]:
        load.wait()
    seq = lax.broadcasted_iota(jnp.int32, (2, 128), 1)
    half = lax.broadcasted_iota(jnp.int32, (1, 256), 1) // 128
    masks = []
    for q in range(2):
        gaps = jnp.sum(
            jnp.where(seq == 16 * y + 8 * q + z, flags[...], 0), axis=1, keepdims=True
        )
        masks.append(jnp.where(half == 0, gaps[0:1], gaps[1:2]) == 1)

    got = xrows.at[c, pl.ds(0, 7)]
    remote(got, got, xb_s, xb_r, sib).wait_recv()
    swap = remote(xrows.at[c], xrows.at[c], xd_s, xd_r, sib)
    swap.start()
    swap.wait_recv()
    row_normed = normalize(xrows[...].reshape(512, 256).astype(F32), rgain[...])
    queries = (mm(row_normed, rin[0]) * DEPTH ** (-0.5)).astype(BF)
    keys = mm(row_normed, rin[1]).astype(BF)
    values = mm(row_normed, rin[2]).astype(BF)
    gates = jax.nn.sigmoid(mm(row_normed, rin[3]))

    totals = [jnp.zeros((256, 256), F32)] * 2
    for g in range(4):
        part = bias.at[g, pl.ds(0, 224)]
        remote(part, part, bb_s.at[g], bb_r.at[g], sib).wait_recv()
        added = mm(natural, bias[g])
        mine = head_lanes(g, 256)
        for q in range(2):
            here = slice(256 * q, 256 * q + 256)
            scores = mm_nt(jnp.where(mine, queries[here], 0), keys[here]) + added
            scores = jnp.where(masks[q], MASKED_SCORE, scores)
            scores = scores - jnp.max(scores, axis=1, keepdims=True)
            totals[q] = totals[q] + mm(
                jnp.exp(scores).astype(BF), value_and_count(mine, values[here])
            )
    for q in range(2):
        gated = totals[q][:, 0:128] / totals[q][:, 128:256] * gates[256 * q : 256 * q + 256]
        gsend[q] = gated.astype(BF).reshape(128, 2, 128)

    lanes = pl.ds(pl.multiple_of(c * 128, 128), 128)
    keep = pltpu.make_async_copy(
        gsend.at[:, me], cols.at[y, :, z, :, lanes], own_sem.at[1]
    )
    keep.start()
    for dz, dy, dc in FAR:
        peer = lax.rem(z + dz, 8) * 16 + lax.rem(y + dy, 8) * 2 + (c if dc == 0 else 1 - c)
        remote(gsend.at[:, peer], cols.at[y, :, z, :, lanes], g_s, g_r, peer).start()

    apart = selector(lambda o: lax.rem(o, 128) * 2 + o // 128, 256)
    together = selector(lambda o: lax.rem(o, 2) * 128 + o // 2, 256)
    masked = jnp.where(z // 4 == 0, flags[0:1, :], flags[1:2, :]) == 1
    residual = mm(apart, xloc[...].reshape(256, 256))
    keep.wait()
    got = gsend.at[:, pl.ds(0, 127)]
    remote(got, got, g_s, g_r, sib).wait_recv()

    gated = pick(apart, cols[...].reshape(256, 256))
    first = (residual + mm(gated, rout[...])).astype(BF).astype(F32)
    normed = normalize(first, cgain[...])
    queries = (mm(normed, cin[:, 0:256]) * DEPTH ** (-0.5)).astype(BF)
    keys = mm(normed, cin[:, 256:512]).astype(BF)
    values = mm(normed, cin[:, 512:768]).astype(BF)
    gates = jax.nn.sigmoid(mm(normed, cin[:, 768:1024]))
    attended = []
    for r in range(2):
        q, t, v = (a[128 * r : 128 * r + 128] for a in (queries, keys, values))
        exps = []
        weights = []
        for h in range(HEADS):
            mine = head_lanes(h, 128, 256)
            scores = mm_nt(jnp.where(mine, q, 0), t)
            scores = jnp.where(masked, MASKED_SCORE, scores)
            scores = scores - jnp.max(scores, axis=1, keepdims=True)
            exps.append(jnp.exp(scores).astype(BF))
            weights.append(value_and_count(mine, v))
        total = mm(jnp.concatenate(exps, axis=1), jnp.concatenate(weights, axis=0))
        attended.append(total[:, 0:256] / total[:, 256:512])
    gated = (jnp.concatenate(attended, axis=0) * gates).astype(BF)
    second = (first + mm(gated, cout[...])).astype(BF).astype(F32)
    hidden = jnp.maximum(mm(normalize(second, tgain[...]), wide[...]), 0.0).astype(BF)
    result = (second + mm(hidden, shrink[...])).astype(BF)
    out_ref[...] = pick(together, result)

    remote(bmid.at[pl.ds(0, 15)], bmid.at[pl.ds(0, 15)], ba_s, ba_r, sib).wait_send()
    remote(xmid.at[pl.ds(0, 120)], xmid.at[pl.ds(0, 120)], xa_s, xa_r, sib).wait_send()
    got = xrows.at[c, pl.ds(0, 7)]
    remote(got, got, xb_s, xb_r, sib).wait_send()
    swap.wait_send()
    for g in range(4):
        part = bias.at[g, pl.ds(0, 224)]
        remote(part, part, bb_s.at[g], bb_r.at[g], sib).wait_send()
    got = gsend.at[:, pl.ds(0, 127)]
    remote(got, got, g_s, g_r, sib).wait_send()


def body(
    aligned_chain_features,
    pair_representation_state,
    gap_block_flags,
    pair_norm_gain,
    pair_head_weight,
    horizontal_scaling_factor,
    row_input_weight,
    horizontal_final_matrix,
    vertical_scaling_factor,
    column_input_weight,
    vertical_final_matrix,
    feedforward_scaling_factor,
    feedforward_widen_matrix,
    feedforward_shrink_matrix,
):
    dma = pltpu.SemaphoreType.DMA
    operands = (
        aligned_chain_features,
        pair_representation_state.reshape(512, 128),
        jnp.transpose(gap_block_flags),
        pair_norm_gain.reshape(1, 128),
        jnp.transpose(pair_head_weight),
        horizontal_scaling_factor.reshape(1, 256),
        row_input_weight,
        horizontal_final_matrix,
        vertical_scaling_factor.reshape(1, 256),
        column_input_weight,
        vertical_final_matrix,
        feedforward_scaling_factor.reshape(1, 256),
        feedforward_widen_matrix,
        feedforward_shrink_matrix,
    )
    copies = [a.shape for a in operands[1:]]
    copies[5] = (4, 256, 128)
    result = pl.pallas_call(
        kernel,
        out_shape=jax.ShapeDtypeStruct((256, 256), BF),
        in_specs=[pl.BlockSpec(memory_space=pl.ANY)] * len(operands),
        out_specs=pl.BlockSpec(memory_space=pltpu.VMEM),
        scratch_shapes=[pltpu.VMEM(n, a.dtype) for n, a in zip(copies, operands[1:])]
        + [
            pltpu.VMEM((2, 16, 128), BF),
            pltpu.VMEM((16, 16, 128), BF),
            pltpu.VMEM((4, 32, 256), BF),
            pltpu.VMEM((4, 256, 256), BF),
            pltpu.VMEM((128, 2, 256), BF),
            pltpu.VMEM((128, 2, 256), BF),
            pltpu.VMEM((8, 32, 256), BF),
            pltpu.VMEM((2, 8, 32, 256), BF),
            pltpu.VMEM((2, 128, 2, 128), BF),
            pltpu.VMEM((8, 2, 8, 2, 256), BF),
            dma((13,)), dma((4,)), dma((2,)), dma, dma, dma((4,)), dma((4,)),
            dma, dma, dma, dma, dma, dma, dma, dma,
        ],
        name="evoformer",
        compiler_params=pltpu.CompilerParams(
            collective_id=0, has_side_effects=True, vmem_limit_bytes=56 << 20
        ),
    )(*operands)
    return result.reshape(128, 2, 256)


def solution(mesh):
    placed = (
        P("dp", "res", None),
        P(("dp", "res"), None, None),
        P("dp", None),
        P(),
        P(),
        P(),
        P(),
        P(),
        P(),
        P(),
        P(),
        P(),
        P(),
        P(),
    )
    return jax.shard_map(
        body, mesh=mesh, in_specs=placed, out_specs=P("dp", "res", None), check_vma=False
    )
```

```python
import jax
import jax.numpy as jnp
from jax import lax
from jax.experimental import pallas as pl
from jax.experimental.pallas import tpu as pltpu
from jax.sharding import PartitionSpec as P

EPSILON = 1e-05
MASKED_SCORE = -1000000000.0
HEADS = 8
DEPTH = 32
BF = jnp.bfloat16
F32 = jnp.float32
MESH = pl.DeviceIdType.MESH
NT = (((1,), (1,)), ((), ()))
FAR_Z = (4, 3, 5, 2, 6, 1, 7)
FAR_K = (8, 7, 9, 6, 10, 5, 11, 4, 12, 3, 13, 2, 14, 1, 15)


def normalize(values, gain):
    centred = values - jnp.mean(values, axis=-1, keepdims=True)
    spread = jnp.mean(centred * centred, axis=-1, keepdims=True)
    return (centred * lax.rsqrt(spread + EPSILON) * gain).astype(BF)


def mm(a, b):
    return jnp.dot(a, b, preferred_element_type=F32)


def mm_nt(a, b):
    return lax.dot_general(a, b, NT, preferred_element_type=F32)


def selector(source_of, rows):
    o = lax.broadcasted_iota(jnp.int32, (rows, rows), 0)
    i = lax.broadcasted_iota(jnp.int32, (rows, rows), 1)
    return jnp.where(source_of(o) == i, 1.0, 0.0).astype(F32).astype(BF)


def pick(one_hot, rows):
    return mm(one_hot, rows).astype(BF)


def head_lanes(h, rows, width=128):
    lane = lax.broadcasted_iota(jnp.int32, (rows, width), 1)
    return lane // DEPTH == h


def value_and_count(mine, values):
    count = jnp.where(mine, 1.0, 0.0).astype(BF)
    return jnp.concatenate([jnp.where(mine, values, 0), count], axis=1)


def remote(src, dst, send, recv, device):
    return pltpu.make_async_remote_copy(
        src_ref=src,
        dst_ref=dst,
        send_sem=send,
        recv_sem=recv,
        device_id={"res": device},
        device_id_type=MESH,
    )


def kernel(
    x_hbm, pair_hbm, flags_hbm, pgain_hbm, pw_hbm, rgain_hbm, rin_hbm, rout_hbm,
    cgain_hbm, cin_hbm, cout_hbm, tgain_hbm, wide_hbm, shrink_hbm,
    out_ref,
    xloc, pair, flags, pgain, pw, rgain, rin, rout, cgain, cin, cout, tgain, wide, shrink,
    bloc, bmid, bsend, bias, xgo, xmid, xsend, xrows, query, gate, gsend, cols,
    load_sem, rin_sem, own_sem, ba_s, ba_r, bb_s, bb_r, xa_s, xa_r, xb_s, xb_r,
    xd_s, xd_r, g_s, g_r,
):
    me = lax.axis_index("res")
    z = me // 16
    k = lax.rem(me, 16)
    y = k // 2
    c = lax.rem(me, 2)
    sib = me + 1 - 2 * c
    place = jnp.where(c == 0, z, y)
    slot = jnp.where(c == 0, y, z)
    line = slot * 2 + c

    def device(p, n):
        return jnp.where(c == 0, p * 16 + n, n // 2 * 16 + p * 2 + lax.rem(n, 2))

    barrier = pltpu.get_barrier_semaphore()

    def greet(peer):
        pl.semaphore_signal(barrier, inc=1, device_id={"res": peer}, device_id_type=MESH)

    for j in FAR_Z:
        greet(lax.rem(z + j, 8) * 16 + k)
        greet(z * 16 + lax.rem(y + j, 8) * 2 + c)
        greet(lax.rem(z + j, 8) * 16 + y * 2 + 1 - c)
        greet(z * 16 + lax.rem(y + j, 8) * 2 + 1 - c)
    greet(sib)

    loads = [
        pltpu.make_async_copy(source, target, load_sem.at[n])
        for n, (source, target) in enumerate((
            (pair_hbm, pair), (pgain_hbm, pgain), (pw_hbm, pw), (x_hbm, xloc),
            (flags_hbm, flags), (rgain_hbm, rgain), (rout_hbm, rout),
            (cgain_hbm, cgain), (cin_hbm, cin), (cout_hbm, cout),
            (tgain_hbm, tgain), (wide_hbm, wide), (shrink_hbm, shrink),
        ))
    ]
    loads += [
        pltpu.make_async_copy(
            rin_hbm.at[:, pl.ds(pl.multiple_of(t * 256 + c * 128, 128), 128)],
            rin.at[t],
            rin_sem.at[t],
        )
        for t in range(4)
    ]
    for load in loads:
        load.start()

    for load in loads[0:3]:
        load.wait()
    normed = normalize(pair[...].astype(F32), pgain[...])
    biases = mm_nt(pw[...], normed)
    for group in range(2):
        heads = biases[4 * group : 4 * group + 4]
        bloc[group] = jnp.concatenate(
            [heads[:, 128 * n : 128 * n + 128] for n in range(4)], axis=0
        ).astype(BF)
    by_n = selector(
        lambda o: device(lax.rem(o, 16) // 2, o // 16) * 2 + lax.rem(o, 2), 256
    )
    loads[3].wait()
    xgo[...] = pick(by_n, xloc[...].reshape(256, 256)).reshape(16, 16, 256)

    pl.semaphore_wait(barrier, 29)

    for j in FAR_K:
        n = lax.rem(line + j, 16)
        remote(xgo.at[n], xmid.at[c, slot], xa_s, xa_r, device(place, n)).start()
    for j in FAR_Z:
        yp = lax.rem(y + j, 8)
        remote(bloc.at[0], bmid.at[k], ba_s, ba_r, z * 16 + yp * 2).start()
        zp = lax.rem(z + j, 8)
        remote(bloc.at[1], bmid.at[z * 2 + c], ba_s, ba_r, zp * 16 + y * 2 + 1).start()

    @pl.when(c == 0)
    def _():
        remote(bloc.at[1], bmid.at[z * 2], ba_s, ba_r, sib).start()

    @pl.when(c == 1)
    def _():
        remote(bloc.at[0], bmid.at[k], ba_s, ba_r, sib).start()

    bmid[line] = bloc[c]
    xmid[c, slot] = xgo[line]

    by_h = selector(
        lambda o: lax.rem(o, 32) // 2 * 16 + lax.rem(o, 2) * 8 + o // 128 * 4
        + lax.rem(o, 128) // 32,
        256,
    )
    by_p = selector(
        lambda o: o // 128 * 128 + lax.rem(o, 16) // 2 * 16 + lax.rem(o, 128) // 16 * 2
        + lax.rem(o, 2),
        256,
    )

    def arrival(residue):
        zz, yy = residue // 32, lax.rem(residue, 32) // 4
        return lax.rem(residue, 2) + jnp.where(
            lax.rem(residue, 4) // 2 == 0, zz * 16 + yy * 2, 128 + yy * 16 + zz * 2
        )

    natural = selector(arrival, 256)
    by_line = selector(
        lambda o: arrival(device(o // 32, lax.rem(o, 32) // 2) * 2 + lax.rem(o, 2)), 256
    )

    def spread(js):
        for j in js:
            remote(
                bsend, bias.at[j], bb_s.at[j], bb_r.at[j], device(lax.rem(place + j, 8), line)
            ).start()

    got = xgo.at[pl.ds(0, 15)]
    remote(got, got, xa_s, xa_r, sib).wait_recv()
    xsend[...] = pick(by_p, xmid[...].reshape(256, 256)).reshape(2, 8, 16, 256)
    for j in FAR_Z:
        zp, yp = lax.rem(z + j, 8), lax.rem(y + j, 8)
        remote(xsend.at[0, zp], xrows.at[c, 0, z], xb_s, xb_r, zp * 16 + k).start()
        remote(xsend.at[1, yp], xrows.at[c, 1, y], xb_s, xb_r, z * 16 + yp * 2 + c).start()
    xrows[c, 0, z] = xsend[0, z]
    xrows[c, 1, y] = xsend[1, y]

    remote(bmid.at[pl.ds(0, 15)], bmid.at[pl.ds(0, 15)], ba_s, ba_r, sib).wait_recv()
    sorted_bias = pick(by_h, bmid[...].reshape(256, 128))
    bsend[...] = jnp.concatenate([sorted_bias[0:128], sorted_bias[128:256]], axis=1)
    spread(FAR_Z)


    for load in loads[4:]:
        load.wait()
    seq = lax.broadcasted_iota(jnp.int32, (2, 128), 1)
    half = lax.broadcasted_iota(jnp.int32, (1, 256), 1) // 128
    masks = []
    for q in range(2):
        gaps = jnp.sum(jnp.where(seq == me - c + q, flags[...], 0), axis=1, keepdims=True)
        masks.append(jnp.where(half == 0, gaps[0:1], gaps[1:2]) == 1)

    got = xgo.at[pl.ds(0, 14)]
    remote(got, got, xb_s, xb_r, sib).wait_recv()
    swap = remote(xrows.at[c], xrows.at[c], xd_s, xd_r, sib)
    swap.start()
    swap.wait_recv()
    keys = []
    values = []
    for q in range(2):
        normed = normalize(xrows[q].reshape(256, 256).astype(F32), rgain[...])
        ordered = pick(natural, normed)
        keys.append(mm(ordered, rin[1]).astype(BF))
        values.append(
            jnp.concatenate([mm(ordered, rin[2]).astype(BF), jnp.ones((256, 128), BF)], axis=1)
        )
        ordered = pick(by_line, normed)
        query[q] = (mm(ordered, rin[0]) * DEPTH ** (-0.5)).astype(BF)
        gate[q] = jax.nn.sigmoid(mm(ordered, rin[3]))

    lanes = pl.ds(pl.multiple_of(c * 128, 128), 128)
    pair_rows = pl.ds(pl.multiple_of(me - c, 2), 2)
    mine = [head_lanes(h, 32) for h in range(4)]
    keep = pltpu.make_async_copy(
        gsend.at[place, :, line], cols.at[pair_rows, :, lanes], own_sem
    )
    for j in (0,) + FAR_Z:
        p = lax.rem(place + 8 - j, 8)
        block = pl.ds(pl.multiple_of(p * 32, 32), 32)
        if j == 0:
            added = bsend[...].reshape(128, 256).astype(F32)
        else:
            remote(bsend, bsend, bb_s.at[j], bb_r.at[j], sib).wait_recv()
            added = bias[j].reshape(128, 256).astype(F32)
        for q in range(2):
            rows = query[q, block, :]
            stack = jnp.concatenate([jnp.where(m, rows, 0) for m in mine], axis=0)
            scores = mm_nt(stack, keys[q]) + added
            scores = jnp.where(masks[q], MASKED_SCORE, scores)
            scores = scores - jnp.max(scores, axis=1, keepdims=True)
            sums = mm(jnp.exp(scores).astype(BF), values[q])
            top = sum(jnp.where(mine[h], sums[32 * h : 32 * h + 32, 0:128], 0.0) for h in range(4))
            count = sum(
                jnp.where(mine[h], sums[32 * h : 32 * h + 32, 128:256], 0.0) for h in range(4)
            )
            gsend[p, q] = (top / count * gate[q, block, :]).astype(BF).reshape(16, 2, 128)
        for m in (8, 7, 9, 6, 10, 5, 11, 4, 12, 3, 13, 2, 14, 1, 15, 0):
            if j == 0 and m == 0:
                keep.start()
                continue
            n = lax.rem(line + m, 16)
            remote(
                gsend.at[p, :, n], cols.at[pair_rows, :, lanes], g_s, g_r, device(p, n)
            ).start()

    apart = selector(lambda o: lax.rem(o, 128) * 2 + o // 128, 256)
    masked = jnp.where(z // 4 == 0, flags[0:1, :], flags[1:2, :]) == 1
    residual = mm(apart, xloc[...].reshape(256, 256))
    keep.wait()
    got = cols.at[pl.ds(0, 127)]
    remote(got, got, g_s, g_r, sib).wait_recv()

    gated = pick(apart, cols[...].reshape(256, 256))
    first = (residual + mm(gated, rout[...])).astype(BF).astype(F32)
    normed = normalize(first, cgain[...])
    queries = (mm(normed, cin[:, 0:256]) * DEPTH ** (-0.5)).astype(BF)
    keys = mm(normed, cin[:, 256:512]).astype(BF)
    values = mm(normed, cin[:, 512:768]).astype(BF)
    gates = jax.nn.sigmoid(mm(normed, cin[:, 768:1024]))
    attended = []
    for r in range(2):
        q, t, v = (a[128 * r : 128 * r + 128] for a in (queries, keys, values))
        exps = []
        weights = []
        for h in range(HEADS):
            these = head_lanes(h, 128, 256)
            scores = mm_nt(jnp.where(these, q, 0), t)
            scores = jnp.where(masked, MASKED_SCORE, scores)
            scores = scores - jnp.max(scores, axis=1, keepdims=True)
            exps.append(jnp.exp(scores).astype(BF))
            weights.append(value_and_count(these, v))
        total = mm(jnp.concatenate(exps, axis=1), jnp.concatenate(weights, axis=0))
        attended.append(total[:, 0:256] / total[:, 256:512])
    gated = (jnp.concatenate(attended, axis=0) * gates).astype(BF)
    second = (first + mm(gated, cout[...])).astype(BF).astype(F32)
    hidden = jnp.maximum(mm(normalize(second, tgain[...]), wide[...]), 0.0).astype(BF)
    together = selector(lambda o: lax.rem(o, 2) * 128 + o // 2, 256)
    out_ref[...] = pick(together, (second + mm(hidden, shrink[...])).astype(BF))

    remote(bmid.at[pl.ds(0, 15)], bmid.at[pl.ds(0, 15)], ba_s, ba_r, sib).wait_send()
    got = xgo.at[pl.ds(0, 15)]
    remote(got, got, xa_s, xa_r, sib).wait_send()
    got = xgo.at[pl.ds(0, 14)]
    remote(got, got, xb_s, xb_r, sib).wait_send()
    swap.wait_send()
    for j in FAR_Z:
        remote(bsend, bsend, bb_s.at[j], bb_r.at[j], sib).wait_send()
    got = cols.at[pl.ds(0, 127)]
    remote(got, got, g_s, g_r, sib).wait_send()


def finish(rows_ref, out_ref):
    together = selector(lambda o: lax.rem(o, 2) * 128 + o // 2, 256)
    out_ref[...] = pick(together, rows_ref[...]).reshape(128, 2, 256)


def body(
    aligned_chain_features,
    pair_representation_state,
    gap_block_flags,
    pair_norm_gain,
    pair_head_weight,
    horizontal_scaling_factor,
    row_input_weight,
    horizontal_final_matrix,
    vertical_scaling_factor,
    column_input_weight,
    vertical_final_matrix,
    feedforward_scaling_factor,
    feedforward_widen_matrix,
    feedforward_shrink_matrix,
):
    dma = pltpu.SemaphoreType.DMA
    vmem = pl.BlockSpec(memory_space=pltpu.VMEM)
    operands = (
        aligned_chain_features,
        pair_representation_state.reshape(512, 128),
        jnp.transpose(gap_block_flags),
        pair_norm_gain.reshape(1, 128),
        jnp.transpose(pair_head_weight),
        horizontal_scaling_factor.reshape(1, 256),
        row_input_weight,
        horizontal_final_matrix,
        vertical_scaling_factor.reshape(1, 256),
        column_input_weight,
        vertical_final_matrix,
        feedforward_scaling_factor.reshape(1, 256),
        feedforward_widen_matrix,
        feedforward_shrink_matrix,
    )
    copies = [a.shape for a in operands]
    copies[6] = (4, 256, 128)
    rows = pl.pallas_call(
        kernel,
        out_shape=pltpu.VMEM((256, 256), BF),
        in_specs=[pl.BlockSpec(memory_space=pl.ANY)] * len(operands),
        out_specs=vmem,
        scratch_shapes=[pltpu.VMEM(n, a.dtype) for n, a in zip(copies, operands)]
        + [
            pltpu.VMEM((2, 16, 128), BF),
            pltpu.VMEM((16, 16, 128), BF),
            pltpu.VMEM((128, 256), BF),
            pltpu.VMEM((8, 128, 256), BF),
            pltpu.VMEM((16, 16, 256), BF),
            pltpu.VMEM((2, 8, 16, 256), BF),
            pltpu.VMEM((2, 8, 16, 256), BF),
            pltpu.VMEM((2, 2, 8, 16, 256), BF),
            pltpu.VMEM((2, 256, 128), BF),
            pltpu.VMEM((2, 256, 128), F32),
            pltpu.VMEM((8, 2, 16, 2, 128), BF),
            pltpu.VMEM((128, 2, 256), BF),
            dma((13,)), dma((4,)), dma, dma, dma, dma((8,)), dma((8,)),
            dma, dma, dma, dma, dma, dma, dma, dma,
        ],
        name="evoformer",
        compiler_params=pltpu.CompilerParams(
            collective_id=0, has_side_effects=True, vmem_limit_bytes=56 << 20
        ),
    )(*operands)
    return rows.reshape(128, 2, 256)


def solution(mesh):
    placed = (
        P("dp", "res", None),
        P(("dp", "res"), None, None),
        P("dp", None),
        P(),
        P(),
        P(),
        P(),
        P(),
        P(),
        P(),
        P(),
        P(),
        P(),
        P(),
    )
    return jax.shard_map(
        body, mesh=mesh, in_specs=placed, out_specs=P("dp", "res", None), check_vma=False
    )
```

```python
import jax
import jax.numpy as jnp
from jax import lax
from jax.experimental import pallas as pl
from jax.experimental.pallas import tpu as pltpu
from jax.sharding import PartitionSpec as P

EPSILON = 1e-05
MASKED_SCORE = -1000000000.0
HEADS = 8
DEPTH = 32
BF = jnp.bfloat16
F32 = jnp.float32
MESH = pl.DeviceIdType.MESH
NT = (((1,), (1,)), ((), ()))
FAR_Z = (4, 3, 5, 2, 6, 1, 7)
FAR_K = (8, 7, 9, 6, 10, 5, 11, 4, 12, 3, 13, 2, 14, 1, 15)


def normalize(values, gain):
    centred = values - jnp.mean(values, axis=-1, keepdims=True)
    spread = jnp.mean(centred * centred, axis=-1, keepdims=True)
    return (centred * lax.rsqrt(spread + EPSILON) * gain).astype(BF)


def mm(a, b):
    return jnp.dot(a, b, preferred_element_type=F32)


def mm_nt(a, b):
    return lax.dot_general(a, b, NT, preferred_element_type=F32)


def selector(source_of, rows):
    o = lax.broadcasted_iota(jnp.int32, (rows, rows), 0)
    i = lax.broadcasted_iota(jnp.int32, (rows, rows), 1)
    return jnp.where(source_of(o) == i, 1.0, 0.0).astype(F32).astype(BF)


def pick(one_hot, rows):
    return mm(one_hot, rows).astype(BF)


def head_lanes(h, rows, width=128):
    lane = lax.broadcasted_iota(jnp.int32, (rows, width), 1)
    return lane // DEPTH == h


def value_and_count(mine, values):
    count = jnp.where(mine, 1.0, 0.0).astype(BF)
    return jnp.concatenate([jnp.where(mine, values, 0), count], axis=1)


def remote(src, dst, send, recv, device):
    return pltpu.make_async_remote_copy(
        src_ref=src,
        dst_ref=dst,
        send_sem=send,
        recv_sem=recv,
        device_id={"res": device},
        device_id_type=MESH,
    )


def kernel(
    x_hbm, pair_hbm, flags_hbm, pgain_hbm, pw_hbm, rgain_hbm, rin_hbm, rout_hbm,
    cgain_hbm, cin_hbm, cout_hbm, tgain_hbm, wide_hbm, shrink_hbm,
    out_ref,
    xloc, pair, flags, pgain, pw, rgain, rin, rout, cgain, cin, cout, tgain, wide, shrink,
    bloc, bmid, bsend, bias, xgo, xmid, xsend, xrows, query, gate, gsend, cols,
    load_sem, rin_sem, own_sem, ba_s, ba_r, bb_s, bb_r, xa_s, xa_r, xb_s, xb_r,
    xd_s, xd_r, g_s, g_r,
):
    me = lax.axis_index("res")
    z = me // 16
    k = lax.rem(me, 16)
    y = k // 2
    c = lax.rem(me, 2)
    sib = me + 1 - 2 * c
    place = jnp.where(c == 0, z, y)
    slot = jnp.where(c == 0, y, z)
    line = slot * 2 + c

    def device(p, n):
        return jnp.where(c == 0, p * 16 + n, n // 2 * 16 + p * 2 + lax.rem(n, 2))

    barrier = pltpu.get_barrier_semaphore()

    def greet(peer):
        pl.semaphore_signal(barrier, inc=1, device_id={"res": peer}, device_id_type=MESH)

    for j in FAR_Z:
        greet(lax.rem(z + j, 8) * 16 + k)
        greet(z * 16 + lax.rem(y + j, 8) * 2 + c)
        greet(lax.rem(z + j, 8) * 16 + y * 2 + 1 - c)
        greet(z * 16 + lax.rem(y + j, 8) * 2 + 1 - c)
    greet(sib)

    loads = [
        pltpu.make_async_copy(source, target, load_sem.at[n])
        for n, (source, target) in enumerate((
            (pair_hbm, pair), (pgain_hbm, pgain), (pw_hbm, pw), (x_hbm, xloc), (rgain_hbm, rgain),
            (flags_hbm, flags), (rout_hbm, rout),
            (cgain_hbm, cgain), (cin_hbm, cin), (cout_hbm, cout),
            (tgain_hbm, tgain), (wide_hbm, wide), (shrink_hbm, shrink),
        ))
    ]
    loads += [
        pltpu.make_async_copy(
            rin_hbm.at[:, pl.ds(pl.multiple_of(t * 256 + c * 128, 128), 128)],
            rin.at[t],
            rin_sem.at[t],
        )
        for t in range(4)
    ]
    for load in loads:
        load.start()

    for load in loads[0:3]:
        load.wait()
    normed = normalize(pair[...].astype(F32), pgain[...])
    biases = mm_nt(pw[...], normed)
    for group in range(2):
        heads = biases[4 * group : 4 * group + 4]
        bloc[group] = jnp.concatenate(
            [heads[:, 128 * n : 128 * n + 128] for n in range(4)], axis=0
        ).astype(BF)
    by_n = selector(
        lambda o: device(lax.rem(o, 16) // 2, o // 16) * 2 + lax.rem(o, 2), 256
    )
    for load in loads[3:5]:
        load.wait()
    normed = normalize(xloc[...].reshape(256, 256).astype(F32), rgain[...])
    xgo[...] = pick(by_n, normed).reshape(16, 16, 256)

    pl.semaphore_wait(barrier, 29)

    for j in FAR_K:
        n = lax.rem(line + j, 16)
        remote(xgo.at[n], xmid.at[c, slot], xa_s, xa_r, device(place, n)).start()
    for j in FAR_Z:
        yp = lax.rem(y + j, 8)
        remote(bloc.at[0], bmid.at[k], ba_s, ba_r, z * 16 + yp * 2).start()
        zp = lax.rem(z + j, 8)
        remote(bloc.at[1], bmid.at[z * 2 + c], ba_s, ba_r, zp * 16 + y * 2 + 1).start()

    @pl.when(c == 0)
    def _():
        remote(bloc.at[1], bmid.at[z * 2], ba_s, ba_r, sib).start()

    @pl.when(c == 1)
    def _():
        remote(bloc.at[0], bmid.at[k], ba_s, ba_r, sib).start()

    bmid[line] = bloc[c]
    xmid[c, slot] = xgo[line]

    by_h = selector(
        lambda o: lax.rem(o, 32) // 2 * 16 + lax.rem(o, 2) * 8 + o // 128 * 4
        + lax.rem(o, 128) // 32,
        256,
    )
    by_p = selector(
        lambda o: o // 128 * 128 + lax.rem(o, 16) // 2 * 16 + lax.rem(o, 128) // 16 * 2
        + lax.rem(o, 2),
        256,
    )

    def arrival(residue):
        zz, yy = residue // 32, lax.rem(residue, 32) // 4
        return lax.rem(residue, 2) + jnp.where(
            lax.rem(residue, 4) // 2 == 0, zz * 16 + yy * 2, 128 + yy * 16 + zz * 2
        )

    natural = selector(arrival, 256)
    by_line = selector(
        lambda o: arrival(device(o // 32, lax.rem(o, 32) // 2) * 2 + lax.rem(o, 2)), 256
    )

    def spread(js):
        for j in js:
            remote(
                bsend, bias.at[j], bb_s.at[j], bb_r.at[j], device(lax.rem(place + j, 8), line)
            ).start()

    got = xgo.at[pl.ds(0, 15)]
    remote(got, got, xa_s, xa_r, sib).wait_recv()
    xsend[...] = pick(by_p, xmid[...].reshape(256, 256)).reshape(2, 8, 16, 256)
    for j in FAR_Z:
        zp, yp = lax.rem(z + j, 8), lax.rem(y + j, 8)
        remote(xsend.at[0, zp], xrows.at[c, 0, z], xb_s, xb_r.at[0], zp * 16 + k).start()
        remote(xsend.at[1, yp], xrows.at[c, 1, y], xb_s, xb_r.at[1], z * 16 + yp * 2 + c).start()
    xrows[c, 0, z] = xsend[0, z]
    xrows[c, 1, y] = xsend[1, y]

    remote(bmid.at[pl.ds(0, 15)], bmid.at[pl.ds(0, 15)], ba_s, ba_r, sib).wait_recv()
    sorted_bias = pick(by_h, bmid[...].reshape(256, 128))
    bsend[...] = jnp.concatenate([sorted_bias[0:128], sorted_bias[128:256]], axis=1)
    spread(FAR_Z)


    for load in loads[5:]:
        load.wait()
    seq = lax.broadcasted_iota(jnp.int32, (2, 128), 1)
    half = lax.broadcasted_iota(jnp.int32, (1, 256), 1) // 128
    masks = []
    for s in (me, sib):
        gaps = jnp.sum(jnp.where(seq == s, flags[...], 0), axis=1, keepdims=True)
        masks.append(jnp.where(half == 0, gaps[0:1], gaps[1:2]) == 1)

    swaps = []
    for n in range(2):
        got = xgo.at[pl.ds(0, 7)]
        remote(got, got, xb_s, xb_r.at[n], sib).wait_recv()
        swaps.append(remote(xrows.at[c, n], xrows.at[c, n], xd_s.at[n], xd_r.at[n], sib))
        swaps[n].start()
    keys = []
    values = []
    for q in range(2):
        if q == 1:
            for swap in swaps:
                swap.wait_recv()
        normed = xrows[c if q == 0 else 1 - c].reshape(256, 256)
        ordered = pick(natural, normed)
        keys.append(mm(ordered, rin[1]).astype(BF))
        values.append(
            jnp.concatenate([mm(ordered, rin[2]).astype(BF), jnp.ones((256, 128), BF)], axis=1)
        )
        ordered = pick(by_line, normed)
        query[q] = (mm(ordered, rin[0]) * DEPTH ** (-0.5)).astype(BF)
        gate[q] = jax.nn.sigmoid(mm(ordered, rin[3]))

    lanes = pl.ds(pl.multiple_of(c * 128, 128), 128)
    pair_rows = pl.ds(pl.multiple_of(me - c, 2), 2)
    mine = [head_lanes(h, 32) for h in range(4)]
    keep = pltpu.make_async_copy(
        gsend.at[place, :, line], cols.at[pair_rows, :, lanes], own_sem
    )
    for pair_of in ((4, 0), (3, 5), (2, 6), (1, 7)):
        places = [lax.rem(place + 8 - j, 8) for j in pair_of]
        blocks = [pl.ds(pl.multiple_of(p * 32, 32), 32) for p in places]
        added = []
        for j in pair_of:
            if j == 0:
                added.append(bsend[...].astype(F32))
            else:
                remote(bsend, bsend, bb_s.at[j], bb_r.at[j], sib).wait_recv()
                added.append(bias[j].astype(F32))
        added = jnp.concatenate(added, axis=0)
        for q in range(2):
            stack = jnp.concatenate(
                [jnp.where(m, query[q, block, :], 0) for block in blocks for m in mine], axis=0
            )
            scores = mm_nt(stack, keys[q]) + added
            scores = jnp.where(masks[q], MASKED_SCORE, scores)
            scores = scores - jnp.max(scores, axis=1, keepdims=True)
            sums = mm(jnp.exp(scores).astype(BF), values[q])
            for n, (p, block) in enumerate(zip(places, blocks)):
                parts = [sums[128 * n + 32 * h : 128 * n + 32 * h + 32] for h in range(4)]
                top = sum(jnp.where(m, part[:, 0:128], 0.0) for m, part in zip(mine, parts))
                count = sum(jnp.where(m, part[:, 128:256], 0.0) for m, part in zip(mine, parts))
                gsend[p, c if q == 0 else 1 - c] = (
                    (top / count * gate[q, block, :]).astype(BF).reshape(16, 2, 128)
                )
        for j, p in zip(pair_of, places):
            for m in (8, 7, 9, 6, 10, 5, 11, 4, 12, 3, 13, 2, 14, 1, 15, 0):
                if j == 0 and m == 0:
                    keep.start()
                    continue
                n = lax.rem(line + m, 16)
                remote(
                    gsend.at[p, :, n], cols.at[pair_rows, :, lanes], g_s, g_r, device(p, n)
                ).start()

    apart = selector(lambda o: lax.rem(o, 128) * 2 + o // 128, 256)
    masked = jnp.where(z // 4 == 0, flags[0:1, :], flags[1:2, :]) == 1
    residual = mm(apart, xloc[...].reshape(256, 256))
    keep.wait()
    got = cols.at[pl.ds(0, 127)]
    remote(got, got, g_s, g_r, sib).wait_recv()

    gated = pick(apart, cols[...].reshape(256, 256))
    first = (residual + mm(gated, rout[...])).astype(BF).astype(F32)
    normed = normalize(first, cgain[...])
    queries = (mm(normed, cin[:, 0:256]) * DEPTH ** (-0.5)).astype(BF)
    keys = mm(normed, cin[:, 256:512]).astype(BF)
    values = mm(normed, cin[:, 512:768]).astype(BF)
    gates = jax.nn.sigmoid(mm(normed, cin[:, 768:1024]))
    attended = []
    for r in range(2):
        q, t, v = (a[128 * r : 128 * r + 128] for a in (queries, keys, values))
        exps = []
        weights = []
        for h in range(HEADS):
            these = head_lanes(h, 128, 256)
            scores = mm_nt(jnp.where(these, q, 0), t)
            scores = jnp.where(masked, MASKED_SCORE, scores)
            scores = scores - jnp.max(scores, axis=1, keepdims=True)
            exps.append(jnp.exp(scores).astype(BF))
            weights.append(value_and_count(these, v))
        total = mm(jnp.concatenate(exps, axis=1), jnp.concatenate(weights, axis=0))
        attended.append(total[:, 0:256] / total[:, 256:512])
    gated = (jnp.concatenate(attended, axis=0) * gates).astype(BF)
    second = (first + mm(gated, cout[...])).astype(BF).astype(F32)
    hidden = jnp.maximum(mm(normalize(second, tgain[...]), wide[...]), 0.0).astype(BF)
    together = selector(lambda o: lax.rem(o, 2) * 128 + o // 2, 256)
    out_ref[...] = pick(together, (second + mm(hidden, shrink[...])).astype(BF))

    remote(bmid.at[pl.ds(0, 15)], bmid.at[pl.ds(0, 15)], ba_s, ba_r, sib).wait_send()
    got = xgo.at[pl.ds(0, 15)]
    remote(got, got, xa_s, xa_r, sib).wait_send()
    got = xgo.at[pl.ds(0, 14)]
    remote(got, got, xb_s, xb_r.at[0], sib).wait_send()
    for swap in swaps:
        swap.wait_send()
    for j in FAR_Z:
        remote(bsend, bsend, bb_s.at[j], bb_r.at[j], sib).wait_send()
    got = cols.at[pl.ds(0, 127)]
    remote(got, got, g_s, g_r, sib).wait_send()


def finish(rows_ref, out_ref):
    together = selector(lambda o: lax.rem(o, 2) * 128 + o // 2, 256)
    out_ref[...] = pick(together, rows_ref[...]).reshape(128, 2, 256)


def body(
    aligned_chain_features,
    pair_representation_state,
    gap_block_flags,
    pair_norm_gain,
    pair_head_weight,
    horizontal_scaling_factor,
    row_input_weight,
    horizontal_final_matrix,
    vertical_scaling_factor,
    column_input_weight,
    vertical_final_matrix,
    feedforward_scaling_factor,
    feedforward_widen_matrix,
    feedforward_shrink_matrix,
):
    dma = pltpu.SemaphoreType.DMA
    vmem = pl.BlockSpec(memory_space=pltpu.VMEM)
    operands = (
        aligned_chain_features,
        pair_representation_state.reshape(512, 128),
        jnp.transpose(gap_block_flags),
        pair_norm_gain.reshape(1, 128),
        jnp.transpose(pair_head_weight),
        horizontal_scaling_factor.reshape(1, 256),
        row_input_weight,
        horizontal_final_matrix,
        vertical_scaling_factor.reshape(1, 256),
        column_input_weight,
        vertical_final_matrix,
        feedforward_scaling_factor.reshape(1, 256),
        feedforward_widen_matrix,
        feedforward_shrink_matrix,
    )
    copies = [a.shape for a in operands]
    copies[6] = (4, 256, 128)
    rows = pl.pallas_call(
        kernel,
        out_shape=pltpu.VMEM((256, 256), BF),
        in_specs=[pl.BlockSpec(memory_space=pl.ANY)] * len(operands),
        out_specs=vmem,
        scratch_shapes=[pltpu.VMEM(n, a.dtype) for n, a in zip(copies, operands)]
        + [
            pltpu.VMEM((2, 16, 128), BF),
            pltpu.VMEM((16, 16, 128), BF),
            pltpu.VMEM((128, 256), BF),
            pltpu.VMEM((8, 128, 256), BF),
            pltpu.VMEM((16, 16, 256), BF),
            pltpu.VMEM((2, 8, 16, 256), BF),
            pltpu.VMEM((2, 8, 16, 256), BF),
            pltpu.VMEM((2, 2, 8, 16, 256), BF),
            pltpu.VMEM((2, 256, 128), BF),
            pltpu.VMEM((2, 256, 128), F32),
            pltpu.VMEM((8, 2, 16, 2, 128), BF),
            pltpu.VMEM((128, 2, 256), BF),
            dma((13,)), dma((4,)), dma, dma, dma, dma((8,)), dma((8,)),
            dma, dma, dma, dma((2,)), dma((2,)), dma((2,)), dma, dma,
        ],
        name="evoformer",
        compiler_params=pltpu.CompilerParams(
            collective_id=0, has_side_effects=True, vmem_limit_bytes=56 << 20
        ),
    )(*operands)
    return rows.reshape(128, 2, 256)


def solution(mesh):
    placed = (
        P("dp", "res", None),
        P(("dp", "res"), None, None),
        P("dp", None),
        P(),
        P(),
        P(),
        P(),
        P(),
        P(),
        P(),
        P(),
        P(),
        P(),
        P(),
    )
    return jax.shard_map(
        body, mesh=mesh, in_specs=placed, out_specs=P("dp", "res", None), check_vma=False
    )
```

```python
import jax
import jax.numpy as jnp
from jax import lax
from jax.experimental import pallas as pl
from jax.experimental.pallas import tpu as pltpu
from jax.sharding import PartitionSpec as P

EPSILON = 1e-05
MASKED_SCORE = -1000000000.0
HEADS = 8
DEPTH = 32
BF = jnp.bfloat16
F32 = jnp.float32
MESH = pl.DeviceIdType.MESH
NT = (((1,), (1,)), ((), ()))
FAR_Z = (4, 3, 5, 2, 6, 1, 7)
FAR_K = (8, 7, 9, 6, 10, 5, 11, 4, 12, 3, 13, 2, 14, 1, 15)


def normalize(values, gain):
    centred = values - jnp.mean(values, axis=-1, keepdims=True)
    spread = jnp.mean(centred * centred, axis=-1, keepdims=True)
    return (centred * lax.rsqrt(spread + EPSILON) * gain).astype(BF)


def mm(a, b):
    return jnp.dot(a, b, preferred_element_type=F32)


def mm_nt(a, b):
    return lax.dot_general(a, b, NT, preferred_element_type=F32)


def selector(source_of, rows):
    o = lax.broadcasted_iota(jnp.int32, (rows, rows), 0)
    i = lax.broadcasted_iota(jnp.int32, (rows, rows), 1)
    return jnp.where(source_of(o) == i, 1.0, 0.0).astype(F32).astype(BF)


def pick(one_hot, rows):
    return mm(one_hot, rows).astype(BF)


def head_lanes(h, rows, width=128):
    lane = lax.broadcasted_iota(jnp.int32, (rows, width), 1)
    return lane // DEPTH == h


def value_and_count(mine, values):
    count = jnp.where(mine, 1.0, 0.0).astype(BF)
    return jnp.concatenate([jnp.where(mine, values, 0), count], axis=1)


def remote(src, dst, send, recv, device):
    return pltpu.make_async_remote_copy(
        src_ref=src,
        dst_ref=dst,
        send_sem=send,
        recv_sem=recv,
        device_id={"res": device},
        device_id_type=MESH,
    )


def kernel(
    x_hbm, pair_hbm, flags_hbm, pgain_hbm, pw_hbm, rgain_hbm, rin_hbm, rout_hbm,
    cgain_hbm, cin_hbm, cout_hbm, tgain_hbm, wide_hbm, shrink_hbm,
    out_ref,
    xloc, pair, flags, pgain, pw, rgain, rin, rout, cgain, cin, cout, tgain, wide, shrink,
    bloc, bmid, bsend, bias, xgo, xmid, xsend, xrows, query, gate, gsend, cols,
    load_sem, rin_sem, own_sem, ba_s, ba_r, bb_s, bb_r, xa_s, xa_r, xb_s, xb_r,
    xd_s, xd_r, g_s, g_r,
):
    me = lax.axis_index("res")
    z = me // 16
    k = lax.rem(me, 16)
    y = k // 2
    c = lax.rem(me, 2)
    sib = me + 1 - 2 * c
    place = jnp.where(c == 0, z, y)
    slot = jnp.where(c == 0, y, z)
    line = slot * 2 + c

    def device(p, n):
        return jnp.where(c == 0, p * 16 + n, n // 2 * 16 + p * 2 + lax.rem(n, 2))

    barrier = pltpu.get_barrier_semaphore()

    def greet(peer):
        pl.semaphore_signal(barrier, inc=1, device_id={"res": peer}, device_id_type=MESH)

    for j in FAR_Z:
        greet(lax.rem(z + j, 8) * 16 + k)
        greet(z * 16 + lax.rem(y + j, 8) * 2 + c)
        greet(lax.rem(z + j, 8) * 16 + y * 2 + 1 - c)
        greet(z * 16 + lax.rem(y + j, 8) * 2 + 1 - c)
    greet(sib)

    loads = [
        pltpu.make_async_copy(source, target, load_sem.at[n])
        for n, (source, target) in enumerate((
            (pair_hbm, pair), (pgain_hbm, pgain), (pw_hbm, pw), (x_hbm, xloc), (rgain_hbm, rgain),
            (flags_hbm, flags), (rout_hbm, rout),
            (cgain_hbm, cgain), (cin_hbm, cin), (cout_hbm, cout),
            (tgain_hbm, tgain), (wide_hbm, wide), (shrink_hbm, shrink),
        ))
    ]
    loads += [
        pltpu.make_async_copy(
            rin_hbm.at[:, pl.ds(pl.multiple_of(t * 256 + c * 128, 128), 128)],
            rin.at[t],
            rin_sem.at[t],
        )
        for t in range(4)
    ]
    for load in loads:
        load.start()

    def arrival(residue):
        zz, yy = residue // 32, lax.rem(residue, 32) // 4
        return lax.rem(residue, 2) + jnp.where(
            lax.rem(residue, 4) // 2 == 0, zz * 16 + yy * 2, 128 + yy * 16 + zz * 2
        )

    column = lax.broadcasted_iota(jnp.int32, (256, 256), 1)
    residue = lax.broadcasted_iota(jnp.int32, (256, 256), 0)
    arranged = jnp.where(arrival(residue) == column, 1.0, 0.0).astype(F32).astype(BF)

    for load in loads[0:3]:
        load.wait()
    normed = normalize(pair[...].astype(F32), pgain[...])
    biases = mm_nt(pw[...], normed).astype(BF)
    biases = [mm(biases[:, 256 * n : 256 * n + 256], arranged) for n in range(2)]
    for group in range(2):
        heads = [rows[4 * group : 4 * group + 4] for rows in biases]
        bloc[group] = jnp.concatenate(
            [rows[:, 128 * n : 128 * n + 128] for rows in heads for n in range(2)], axis=0
        ).astype(BF)
    by_n = selector(
        lambda o: device(lax.rem(o, 16) // 2, o // 16) * 2 + lax.rem(o, 2), 256
    )
    for load in loads[3:5]:
        load.wait()
    normed = normalize(xloc[...].reshape(256, 256).astype(F32), rgain[...])
    xgo[...] = pick(by_n, normed).reshape(16, 16, 256)

    pl.semaphore_wait(barrier, 29)

    for j in FAR_K:
        n = lax.rem(line + j, 16)
        remote(xgo.at[n], xmid.at[c, slot], xa_s, xa_r, device(place, n)).start()
    for j in FAR_Z:
        yp = lax.rem(y + j, 8)
        remote(bloc.at[0], bmid.at[k], ba_s, ba_r, z * 16 + yp * 2).start()
        zp = lax.rem(z + j, 8)
        remote(bloc.at[1], bmid.at[z * 2 + c], ba_s, ba_r, zp * 16 + y * 2 + 1).start()

    @pl.when(c == 0)
    def _():
        remote(bloc.at[1], bmid.at[z * 2], ba_s, ba_r, sib).start()

    @pl.when(c == 1)
    def _():
        remote(bloc.at[0], bmid.at[k], ba_s, ba_r, sib).start()

    bmid[line] = bloc[c]
    xmid[c, slot] = xgo[line]

    by_h = selector(
        lambda o: lax.rem(o, 32) // 2 * 16 + lax.rem(o, 2) * 8 + o // 128 * 4
        + lax.rem(o, 128) // 32,
        256,
    )
    by_p = selector(
        lambda o: o // 128 * 128 + lax.rem(o, 16) // 2 * 16 + lax.rem(o, 128) // 16 * 2
        + lax.rem(o, 2),
        256,
    )
    by_line = selector(
        lambda o: arrival(device(o // 32, lax.rem(o, 32) // 2) * 2 + lax.rem(o, 2)), 256
    )

    def spread(js):
        for j in js:
            remote(
                bsend, bias.at[j], bb_s.at[j], bb_r.at[j], device(lax.rem(place + j, 8), line)
            ).start()

    got = xgo.at[pl.ds(0, 15)]
    remote(got, got, xa_s, xa_r, sib).wait_recv()
    xsend[...] = pick(by_p, xmid[...].reshape(256, 256)).reshape(2, 8, 16, 256)
    for j in FAR_Z:
        zp, yp = lax.rem(z + j, 8), lax.rem(y + j, 8)
        remote(xsend.at[0, zp], xrows.at[c, 0, z], xb_s, xb_r.at[0], zp * 16 + k).start()
        remote(xsend.at[1, yp], xrows.at[c, 1, y], xb_s, xb_r.at[1], z * 16 + yp * 2 + c).start()
    xrows[c, 0, z] = xsend[0, z]
    xrows[c, 1, y] = xsend[1, y]

    remote(bmid.at[pl.ds(0, 15)], bmid.at[pl.ds(0, 15)], ba_s, ba_r, sib).wait_recv()
    sorted_bias = pick(by_h, bmid[...].reshape(256, 128))
    bsend[...] = jnp.concatenate([sorted_bias[0:128], sorted_bias[128:256]], axis=1)
    spread(FAR_Z)


    for load in loads[5:]:
        load.wait()
    seq = lax.broadcasted_iota(jnp.int32, (2, 128), 1)
    lane = lax.broadcasted_iota(jnp.int32, (1, 256), 1)
    half = jnp.where(lane < 128, lane // 16, lax.rem(lane, 16) // 2) // 4
    masks = []
    for s in (me, sib):
        gaps = jnp.sum(jnp.where(seq == s, flags[...], 0), axis=1, keepdims=True)
        masks.append(jnp.where(half == 0, gaps[0:1], gaps[1:2]) == 1)

    swaps = []
    for n in range(2):
        got = xgo.at[pl.ds(0, 7)]
        remote(got, got, xb_s, xb_r.at[n], sib).wait_recv()
        swaps.append(remote(xrows.at[c, n], xrows.at[c, n], xd_s.at[n], xd_r.at[n], sib))
        swaps[n].start()
    keys = []
    values = []
    for q in range(2):
        if q == 1:
            for swap in swaps:
                swap.wait_recv()
        normed = xrows[c if q == 0 else 1 - c].reshape(256, 256)
        keys.append(mm(normed, rin[1]).astype(BF))
        values.append(
            jnp.concatenate([mm(normed, rin[2]).astype(BF), jnp.ones((256, 128), BF)], axis=1)
        )
        ordered = pick(by_line, normed)
        query[q] = (mm(ordered, rin[0]) * DEPTH ** (-0.5)).astype(BF)
        gate[q] = jax.nn.sigmoid(mm(ordered, rin[3]))

    mine = [head_lanes(h, 32) for h in range(4)]
    keep = pltpu.make_async_copy(
        gsend.at[place, line], cols.at[c, me // 2], own_sem
    )
    for pair_of in ((4, 0), (3, 5), (2, 6), (1, 7)):
        places = [lax.rem(place + 8 - j, 8) for j in pair_of]
        blocks = [pl.ds(pl.multiple_of(p * 32, 32), 32) for p in places]
        added = []
        for j in pair_of:
            if j > 0:
                remote(bsend, bsend, bb_s.at[j], bb_r.at[j], sib).wait_recv()
            added.append((bias[j] if j > 0 else bsend[...]).astype(F32))
        added = jnp.concatenate(added, axis=0)
        for q in range(2):
            stack = jnp.concatenate(
                [jnp.where(m, query[q, block, :], 0) for block in blocks for m in mine], axis=0
            )
            scores = mm_nt(stack, keys[q]) + added
            scores = jnp.where(masks[q], MASKED_SCORE, scores)
            scores = scores - jnp.max(scores, axis=1, keepdims=True)
            sums = mm(jnp.exp(scores).astype(BF), values[q])
            for n, (p, block) in enumerate(zip(places, blocks)):
                parts = [sums[128 * n + 32 * h : 128 * n + 32 * h + 32] for h in range(4)]
                top = sum(jnp.where(m, part[:, 0:128], 0.0) for m, part in zip(mine, parts))
                count = sum(jnp.where(m, part[:, 128:256], 0.0) for m, part in zip(mine, parts))
                gsend[p, :, c if q == 0 else 1 - c] = (
                    (top / count * gate[q, block, :]).astype(BF).reshape(16, 2, 128)
                )
        for j, p in zip(pair_of, places):
            for m in (8, 7, 9, 6, 10, 5, 11, 4, 12, 3, 13, 2, 14, 1, 15, 0):
                if j == 0 and m == 0:
                    keep.start()
                    continue
                n = lax.rem(line + m, 16)
                remote(
                    gsend.at[p, n], cols.at[c, me // 2], g_s, g_r, device(p, n)
                ).start()

    apart = selector(lambda o: lax.rem(o, 128) * 2 + o // 128, 256)
    masked = jnp.where(z // 4 == 0, flags[0:1, :], flags[1:2, :]) == 1
    residual = mm(apart, xloc[...].reshape(256, 256))
    keep.wait()
    got = xloc.at[pl.ds(0, 127)]
    remote(got, got, g_s, g_r, sib).wait_recv()

    halves = [cols[group].reshape(256, 128) for group in range(2)]
    gated = pick(apart, jnp.concatenate(halves, axis=1))
    first = (residual + mm(gated, rout[...])).astype(BF).astype(F32)
    normed = normalize(first, cgain[...])
    queries = (mm(normed, cin[:, 0:256]) * DEPTH ** (-0.5)).astype(BF)
    keys = mm(normed, cin[:, 256:512]).astype(BF)
    values = mm(normed, cin[:, 512:768]).astype(BF)
    gates = jax.nn.sigmoid(mm(normed, cin[:, 768:1024]))
    attended = []
    for r in range(2):
        q, t, v = (a[128 * r : 128 * r + 128] for a in (queries, keys, values))
        exps = []
        weights = []
        for h in range(HEADS):
            these = head_lanes(h, 128, 256)
            scores = mm_nt(jnp.where(these, q, 0), t)
            scores = jnp.where(masked, MASKED_SCORE, scores)
            scores = scores - jnp.max(scores, axis=1, keepdims=True)
            exps.append(jnp.exp(scores).astype(BF))
            weights.append(value_and_count(these, v))
        total = mm(jnp.concatenate(exps, axis=1), jnp.concatenate(weights, axis=0))
        attended.append(total[:, 0:256] / total[:, 256:512])
    gated = (jnp.concatenate(attended, axis=0) * gates).astype(BF)
    second = (first + mm(gated, cout[...])).astype(BF).astype(F32)
    hidden = jnp.maximum(mm(normalize(second, tgain[...]), wide[...]), 0.0).astype(BF)
    out_ref[...] = (second + mm(hidden, shrink[...])).astype(BF)

    remote(bmid.at[pl.ds(0, 15)], bmid.at[pl.ds(0, 15)], ba_s, ba_r, sib).wait_send()
    got = xgo.at[pl.ds(0, 15)]
    remote(got, got, xa_s, xa_r, sib).wait_send()
    got = xgo.at[pl.ds(0, 14)]
    remote(got, got, xb_s, xb_r.at[0], sib).wait_send()
    for swap in swaps:
        swap.wait_send()
    for j in FAR_Z:
        remote(bsend, bsend, bb_s.at[j], bb_r.at[j], sib).wait_send()
    got = xloc.at[pl.ds(0, 127)]
    remote(got, got, g_s, g_r, sib).wait_send()


def finish(rows_ref, out_ref):
    together = selector(lambda o: lax.rem(o, 2) * 128 + o // 2, 256)
    out_ref[...] = pick(together, rows_ref[...]).reshape(128, 2, 256)


def body(
    aligned_chain_features,
    pair_representation_state,
    gap_block_flags,
    pair_norm_gain,
    pair_head_weight,
    horizontal_scaling_factor,
    row_input_weight,
    horizontal_final_matrix,
    vertical_scaling_factor,
    column_input_weight,
    vertical_final_matrix,
    feedforward_scaling_factor,
    feedforward_widen_matrix,
    feedforward_shrink_matrix,
):
    dma = pltpu.SemaphoreType.DMA
    vmem = pl.BlockSpec(memory_space=pltpu.VMEM)
    operands = (
        aligned_chain_features,
        pair_representation_state.reshape(512, 128),
        jnp.transpose(gap_block_flags),
        pair_norm_gain.reshape(1, 128),
        jnp.transpose(pair_head_weight),
        horizontal_scaling_factor.reshape(1, 256),
        row_input_weight,
        horizontal_final_matrix,
        vertical_scaling_factor.reshape(1, 256),
        column_input_weight,
        vertical_final_matrix,
        feedforward_scaling_factor.reshape(1, 256),
        feedforward_widen_matrix,
        feedforward_shrink_matrix,
    )
    copies = [a.shape for a in operands]
    copies[6] = (4, 256, 128)
    rows = pl.pallas_call(
        kernel,
        out_shape=pltpu.VMEM((256, 256), BF),
        in_specs=[pl.BlockSpec(memory_space=pl.ANY)] * len(operands),
        out_specs=vmem,
        scratch_shapes=[pltpu.VMEM(n, a.dtype) for n, a in zip(copies, operands)]
        + [
            pltpu.VMEM((2, 16, 128), BF),
            pltpu.VMEM((16, 16, 128), BF),
            pltpu.VMEM((128, 256), BF),
            pltpu.VMEM((8, 128, 256), BF),
            pltpu.VMEM((16, 16, 256), BF),
            pltpu.VMEM((2, 8, 16, 256), BF),
            pltpu.VMEM((2, 8, 16, 256), BF),
            pltpu.VMEM((2, 2, 8, 16, 256), BF),
            pltpu.VMEM((2, 256, 128), BF),
            pltpu.VMEM((2, 256, 128), F32),
            pltpu.VMEM((8, 16, 2, 2, 128), BF),
            pltpu.VMEM((2, 64, 2, 2, 128), BF),
            dma((13,)), dma((4,)), dma, dma, dma, dma((8,)), dma((8,)),
            dma, dma, dma, dma((2,)), dma((2,)), dma((2,)), dma, dma,
        ],
        name="evoformer",
        compiler_params=pltpu.CompilerParams(
            collective_id=0, has_side_effects=True, vmem_limit_bytes=56 << 20
        ),
    )(*operands)
    return jnp.transpose(rows.reshape(2, 128, 256), (1, 0, 2))


def solution(mesh):
    placed = (
        P("dp", "res", None),
        P(("dp", "res"), None, None),
        P("dp", None),
        P(),
        P(),
        P(),
        P(),
        P(),
        P(),
        P(),
        P(),
        P(),
        P(),
        P(),
    )
    return jax.shard_map(
        body, mesh=mesh, in_specs=placed, out_specs=P("dp", "res", None), check_vma=False
    )
```

```python
import jax
import jax.numpy as jnp
from jax import lax
from jax.experimental import pallas as pl
from jax.experimental.pallas import tpu as pltpu
from jax.sharding import PartitionSpec as P

EPSILON = 1e-05
MASKED_SCORE = -1000000000.0
HEADS = 8
DEPTH = 32
BF = jnp.bfloat16
F32 = jnp.float32
MESH = pl.DeviceIdType.MESH
NT = (((1,), (1,)), ((), ()))
FAR_Z = (4, 3, 5, 2, 6, 1, 7)
FAR_K = (8, 7, 9, 6, 10, 5, 11, 4, 12, 3, 13, 2, 14, 1, 15)


def normalize(values, gain):
    centred = values - jnp.mean(values, axis=-1, keepdims=True)
    spread = jnp.mean(centred * centred, axis=-1, keepdims=True)
    return (centred * lax.rsqrt(spread + EPSILON) * gain).astype(BF)


def mm(a, b):
    return jnp.dot(a, b, preferred_element_type=F32)


def mm_nt(a, b):
    return lax.dot_general(a, b, NT, preferred_element_type=F32)


def selector(source_of, rows):
    o = lax.broadcasted_iota(jnp.int32, (rows, rows), 0)
    i = lax.broadcasted_iota(jnp.int32, (rows, rows), 1)
    return jnp.where(source_of(o) == i, 1.0, 0.0).astype(F32).astype(BF)


def pick(one_hot, rows):
    return mm(one_hot, rows).astype(BF)


def head_lanes(h, rows, width=128):
    lane = lax.broadcasted_iota(jnp.int32, (rows, width), 1)
    return lane // DEPTH == h


def value_and_count(mine, values):
    count = jnp.where(mine, 1.0, 0.0).astype(BF)
    return jnp.concatenate([jnp.where(mine, values, 0), count], axis=1)


def remote(src, dst, send, recv, device):
    return pltpu.make_async_remote_copy(
        src_ref=src,
        dst_ref=dst,
        send_sem=send,
        recv_sem=recv,
        device_id={"res": device},
        device_id_type=MESH,
    )


def kernel(
    x_hbm, pair_hbm, flags_hbm, pgain_hbm, pw_hbm, rgain_hbm, rin_hbm, rout_hbm,
    cgain_hbm, cin_hbm, cout_hbm, tgain_hbm, wide_hbm, shrink_hbm,
    out_ref,
    xloc, pair, flags, pgain, pw, rgain, rin, rout, cgain, cin, cout, tgain, wide, shrink,
    bloc, bmid, bsend, bias, xgo, xmid, xsend, xrows, query, gate, gsend, cols,
    load_sem, rin_sem, own_sem, ba_s, ba_r, bb_s, bb_r, xa_s, xa_r, xb_s, xb_r,
    xd_s, xd_r, g_s, g_r,
):
    me = lax.axis_index("res")
    z = me // 16
    k = lax.rem(me, 16)
    y = k // 2
    c = lax.rem(me, 2)
    sib = me + 1 - 2 * c
    place = jnp.where(c == 0, z, y)
    slot = jnp.where(c == 0, y, z)
    line = slot * 2 + c

    def device(p, n):
        return jnp.where(c == 0, p * 16 + n, n // 2 * 16 + p * 2 + lax.rem(n, 2))

    barrier = pltpu.get_barrier_semaphore()

    def greet(peer):
        pl.semaphore_signal(barrier, inc=1, device_id={"res": peer}, device_id_type=MESH)

    for j in FAR_Z:
        greet(lax.rem(z + j, 8) * 16 + k)
        greet(z * 16 + lax.rem(y + j, 8) * 2 + c)
        greet(lax.rem(z + j, 8) * 16 + y * 2 + 1 - c)
        greet(z * 16 + lax.rem(y + j, 8) * 2 + 1 - c)
    greet(sib)

    loads = [
        pltpu.make_async_copy(source, target, load_sem.at[n])
        for n, (source, target) in enumerate((
            (pair_hbm, pair), (pgain_hbm, pgain), (pw_hbm, pw), (x_hbm, xloc), (rgain_hbm, rgain),
            (flags_hbm, flags), (rout_hbm, rout),
            (cgain_hbm, cgain), (cin_hbm, cin), (cout_hbm, cout),
            (tgain_hbm, tgain), (wide_hbm, wide), (shrink_hbm, shrink),
        ))
    ]
    loads += [
        pltpu.make_async_copy(
            rin_hbm.at[:, pl.ds(pl.multiple_of(t * 256 + c * 128, 128), 128)],
            rin.at[t],
            rin_sem.at[t],
        )
        for t in range(4)
    ]
    for load in loads[:5]:
        load.start()

    def arrival(residue):
        zz, yy = residue // 32, lax.rem(residue, 32) // 4
        return lax.rem(residue, 2) + jnp.where(
            lax.rem(residue, 4) // 2 == 0, zz * 16 + yy * 2, 128 + yy * 16 + zz * 2
        )

    column = lax.broadcasted_iota(jnp.int32, (256, 256), 1)
    residue = lax.broadcasted_iota(jnp.int32, (256, 256), 0)
    arranged = jnp.where(arrival(residue) == column, 1.0, 0.0).astype(F32).astype(BF)

    for load in loads[0:3]:
        load.wait()
    normed = normalize(pair[...].astype(F32), pgain[...])
    biases = mm_nt(pw[...], normed).astype(BF)
    biases = [mm(biases[:, 256 * n : 256 * n + 256], arranged) for n in range(2)]
    for group in range(2):
        heads = [rows[4 * group : 4 * group + 4] for rows in biases]
        bloc[group] = jnp.concatenate(
            [rows[:, 128 * n : 128 * n + 128] for rows in heads for n in range(2)], axis=0
        ).astype(BF)
    by_n = selector(
        lambda o: device(lax.rem(o, 16) // 2, o // 16) * 2 + lax.rem(o, 2), 256
    )
    for load in loads[3:5]:
        load.wait()
    normed = normalize(xloc[...].reshape(256, 256).astype(F32), rgain[...])
    xgo[...] = pick(by_n, normed).reshape(16, 16, 256)

    pl.semaphore_wait(barrier, 29)

    for j in FAR_K:
        n = lax.rem(line + j, 16)
        remote(xgo.at[n], xmid.at[c, slot], xa_s, xa_r, device(place, n)).start()
    for j in FAR_Z:
        yp = lax.rem(y + j, 8)
        remote(bloc.at[0], bmid.at[k], ba_s, ba_r, z * 16 + yp * 2).start()
        zp = lax.rem(z + j, 8)
        remote(bloc.at[1], bmid.at[z * 2 + c], ba_s, ba_r, zp * 16 + y * 2 + 1).start()

    @pl.when(c == 0)
    def _():
        remote(bloc.at[1], bmid.at[z * 2], ba_s, ba_r, sib).start()

    @pl.when(c == 1)
    def _():
        remote(bloc.at[0], bmid.at[k], ba_s, ba_r, sib).start()

    for load in loads[5:]:
        load.start()
    bmid[line] = bloc[c]
    xmid[c, slot] = xgo[line]

    by_h = selector(
        lambda o: lax.rem(o, 32) // 2 * 16 + lax.rem(o, 2) * 8 + o // 128 * 4
        + lax.rem(o, 128) // 32,
        256,
    )
    by_p = selector(
        lambda o: o // 128 * 128 + lax.rem(o, 16) // 2 * 16 + lax.rem(o, 128) // 16 * 2
        + lax.rem(o, 2),
        256,
    )
    by_line = selector(
        lambda o: arrival(device(o // 32, lax.rem(o, 32) // 2) * 2 + lax.rem(o, 2)), 256
    )

    def spread(js):
        for j in js:
            remote(
                bsend, bias.at[j], bb_s.at[j], bb_r.at[j], device(lax.rem(place + j, 8), line)
            ).start()

    got = xgo.at[pl.ds(0, 15)]
    remote(got, got, xa_s, xa_r, sib).wait_recv()
    xsend[...] = pick(by_p, xmid[...].reshape(256, 256)).reshape(2, 8, 16, 256)
    for j in FAR_Z:
        zp, yp = lax.rem(z + j, 8), lax.rem(y + j, 8)
        remote(xsend.at[0, zp], xrows.at[c, 0, z], xb_s, xb_r.at[0], zp * 16 + k).start()
        remote(xsend.at[1, yp], xrows.at[c, 1, y], xb_s, xb_r.at[1], z * 16 + yp * 2 + c).start()
    xrows[c, 0, z] = xsend[0, z]
    xrows[c, 1, y] = xsend[1, y]

    remote(bmid.at[pl.ds(0, 15)], bmid.at[pl.ds(0, 15)], ba_s, ba_r, sib).wait_recv()
    sorted_bias = pick(by_h, bmid[...].reshape(256, 128))
    bsend[...] = jnp.concatenate([sorted_bias[0:128], sorted_bias[128:256]], axis=1)
    spread(FAR_Z)


    for load in loads[5:]:
        load.wait()
    seq = lax.broadcasted_iota(jnp.int32, (2, 128), 1)
    lane = lax.broadcasted_iota(jnp.int32, (1, 256), 1)
    half = jnp.where(lane < 128, lane // 16, lax.rem(lane, 16) // 2) // 4
    masks = []
    for s in (me, sib):
        gaps = jnp.sum(jnp.where(seq == s, flags[...], 0), axis=1, keepdims=True)
        masks.append(jnp.where(half == 0, gaps[0:1], gaps[1:2]) == 1)

    swaps = []
    for n in range(2):
        got = xgo.at[pl.ds(0, 7)]
        remote(got, got, xb_s, xb_r.at[n], sib).wait_recv()
        swaps.append(remote(xrows.at[c, n], xrows.at[c, n], xd_s.at[n], xd_r.at[n], sib))
        swaps[n].start()
    keys = []
    values = []
    for q in range(2):
        if q == 1:
            for swap in swaps:
                swap.wait_recv()
        normed = xrows[c if q == 0 else 1 - c].reshape(256, 256)
        keys.append(mm(normed, rin[1]).astype(BF))
        values.append(
            jnp.concatenate([mm(normed, rin[2]).astype(BF), jnp.ones((256, 128), BF)], axis=1)
        )
        ordered = pick(by_line, normed)
        query[q] = (mm(ordered, rin[0]) * DEPTH ** (-0.5)).astype(BF)
        gate[q] = jax.nn.sigmoid(mm(ordered, rin[3]))

    mine = [head_lanes(h, 32) for h in range(4)]
    keep = pltpu.make_async_copy(
        gsend.at[place, line], cols.at[c, me // 2], own_sem
    )
    for pair_of in ((4, 0), (3, 5), (2, 6), (1, 7)):
        places = [lax.rem(place + 8 - j, 8) for j in pair_of]
        blocks = [pl.ds(pl.multiple_of(p * 32, 32), 32) for p in places]
        added = []
        for j in pair_of:
            if j > 0:
                remote(bsend, bsend, bb_s.at[j], bb_r.at[j], sib).wait_recv()
            added.append((bias[j] if j > 0 else bsend[...]).astype(F32))
        added = jnp.concatenate(added, axis=0)
        for q in range(2):
            stack = jnp.concatenate(
                [jnp.where(m, query[q, block, :], 0) for block in blocks for m in mine], axis=0
            )
            scores = mm_nt(stack, keys[q]) + added
            scores = jnp.where(masks[q], MASKED_SCORE, scores)
            scores = scores - jnp.max(scores, axis=1, keepdims=True)
            sums = mm(jnp.exp(scores).astype(BF), values[q])
            for n, (p, block) in enumerate(zip(places, blocks)):
                parts = [sums[128 * n + 32 * h : 128 * n + 32 * h + 32] for h in range(4)]
                top = sum(jnp.where(m, part[:, 0:128], 0.0) for m, part in zip(mine, parts))
                count = sum(jnp.where(m, part[:, 128:256], 0.0) for m, part in zip(mine, parts))
                gsend[p, :, c if q == 0 else 1 - c] = (
                    (top / count * gate[q, block, :]).astype(BF).reshape(16, 2, 128)
                )
        for j, p in zip(pair_of, places):
            for m in (8, 7, 9, 6, 10, 5, 11, 4, 12, 3, 13, 2, 14, 1, 15, 0):
                if j == 0 and m == 0:
                    keep.start()
                    continue
                n = lax.rem(line + m, 16)
                remote(
                    gsend.at[p, n], cols.at[c, me // 2], g_s, g_r, device(p, n)
                ).start()

    apart = selector(lambda o: lax.rem(o, 128) * 2 + o // 128, 256)
    masked = jnp.where(z // 4 == 0, flags[0:1, :], flags[1:2, :]) == 1
    residual = mm(apart, xloc[...].reshape(256, 256))
    keep.wait()
    got = xloc.at[pl.ds(0, 127)]
    remote(got, got, g_s, g_r, sib).wait_recv()

    halves = [cols[group].reshape(256, 128) for group in range(2)]
    gated = pick(apart, jnp.concatenate(halves, axis=1))
    first = (residual + mm(gated, rout[...])).astype(BF).astype(F32)
    normed = normalize(first, cgain[...])
    queries = (mm(normed, cin[:, 0:256]) * DEPTH ** (-0.5)).astype(BF)
    keys = mm(normed, cin[:, 256:512]).astype(BF)
    values = mm(normed, cin[:, 512:768]).astype(BF)
    gates = jax.nn.sigmoid(mm(normed, cin[:, 768:1024]))
    attended = []
    for r in range(2):
        q, t, v = (a[128 * r : 128 * r + 128] for a in (queries, keys, values))
        exps = []
        weights = []
        for h in range(HEADS):
            these = head_lanes(h, 128, 256)
            scores = mm_nt(jnp.where(these, q, 0), t)
            scores = jnp.where(masked, MASKED_SCORE, scores)
            scores = scores - jnp.max(scores, axis=1, keepdims=True)
            exps.append(jnp.exp(scores).astype(BF))
            weights.append(value_and_count(these, v))
        total = mm(jnp.concatenate(exps, axis=1), jnp.concatenate(weights, axis=0))
        attended.append(total[:, 0:256] / total[:, 256:512])
    gated = (jnp.concatenate(attended, axis=0) * gates).astype(BF)
    second = (first + mm(gated, cout[...])).astype(BF).astype(F32)
    hidden = jnp.maximum(mm(normalize(second, tgain[...]), wide[...]), 0.0).astype(BF)
    out_ref[...] = (second + mm(hidden, shrink[...])).astype(BF)

    remote(bmid.at[pl.ds(0, 15)], bmid.at[pl.ds(0, 15)], ba_s, ba_r, sib).wait_send()
    got = xgo.at[pl.ds(0, 15)]
    remote(got, got, xa_s, xa_r, sib).wait_send()
    got = xgo.at[pl.ds(0, 14)]
    remote(got, got, xb_s, xb_r.at[0], sib).wait_send()
    for swap in swaps:
        swap.wait_send()
    for j in FAR_Z:
        remote(bsend, bsend, bb_s.at[j], bb_r.at[j], sib).wait_send()
    got = xloc.at[pl.ds(0, 127)]
    remote(got, got, g_s, g_r, sib).wait_send()


def finish(rows_ref, out_ref):
    together = selector(lambda o: lax.rem(o, 2) * 128 + o // 2, 256)
    out_ref[...] = pick(together, rows_ref[...]).reshape(128, 2, 256)


def body(
    aligned_chain_features,
    pair_representation_state,
    gap_block_flags,
    pair_norm_gain,
    pair_head_weight,
    horizontal_scaling_factor,
    row_input_weight,
    horizontal_final_matrix,
    vertical_scaling_factor,
    column_input_weight,
    vertical_final_matrix,
    feedforward_scaling_factor,
    feedforward_widen_matrix,
    feedforward_shrink_matrix,
):
    dma = pltpu.SemaphoreType.DMA
    vmem = pl.BlockSpec(memory_space=pltpu.VMEM)
    operands = (
        aligned_chain_features,
        pair_representation_state.reshape(512, 128),
        jnp.transpose(gap_block_flags),
        pair_norm_gain.reshape(1, 128),
        jnp.transpose(pair_head_weight),
        horizontal_scaling_factor.reshape(1, 256),
        row_input_weight,
        horizontal_final_matrix,
        vertical_scaling_factor.reshape(1, 256),
        column_input_weight,
        vertical_final_matrix,
        feedforward_scaling_factor.reshape(1, 256),
        feedforward_widen_matrix,
        feedforward_shrink_matrix,
    )
    copies = [a.shape for a in operands]
    copies[6] = (4, 256, 128)
    rows = pl.pallas_call(
        kernel,
        out_shape=pltpu.VMEM((256, 256), BF),
        in_specs=[pl.BlockSpec(memory_space=pl.ANY)] * len(operands),
        out_specs=vmem,
        scratch_shapes=[pltpu.VMEM(n, a.dtype) for n, a in zip(copies, operands)]
        + [
            pltpu.VMEM((2, 16, 128), BF),
            pltpu.VMEM((16, 16, 128), BF),
            pltpu.VMEM((128, 256), BF),
            pltpu.VMEM((8, 128, 256), BF),
            pltpu.VMEM((16, 16, 256), BF),
            pltpu.VMEM((2, 8, 16, 256), BF),
            pltpu.VMEM((2, 8, 16, 256), BF),
            pltpu.VMEM((2, 2, 8, 16, 256), BF),
            pltpu.VMEM((2, 256, 128), BF),
            pltpu.VMEM((2, 256, 128), F32),
            pltpu.VMEM((8, 16, 2, 2, 128), BF),
            pltpu.VMEM((2, 64, 2, 2, 128), BF),
            dma((13,)), dma((4,)), dma, dma, dma, dma((8,)), dma((8,)),
            dma, dma, dma, dma((2,)), dma((2,)), dma((2,)), dma, dma,
        ],
        name="evoformer",
        compiler_params=pltpu.CompilerParams(
            collective_id=0, has_side_effects=True, vmem_limit_bytes=56 << 20
        ),
    )(*operands)
    return jnp.transpose(rows.reshape(2, 128, 256), (1, 0, 2))


def solution(mesh):
    placed = (
        P("dp", "res", None),
        P(("dp", "res"), None, None),
        P("dp", None),
        P(),
        P(),
        P(),
        P(),
        P(),
        P(),
        P(),
        P(),
        P(),
        P(),
        P(),
    )
    return jax.shard_map(
        body, mesh=mesh, in_specs=placed, out_specs=P("dp", "res", None), check_vma=False
    )
```
